512 devices in a mesh: gx: 8 (over y), gy: 8 (over z_hi, core), gz: 8 (over x, z_lo).
Axes of the slice: x: 4, y: 8, z: 8 (z_hi: 4, z_lo: 2; z = z_hi * 2 + z_lo), core: 2. Of those that a mesh axis runs over, the one named last changes fastest.
Arguments:
- volume: bfloat16 [64, 256, 128, 32], P('gx', 'gy', 'gz'), may hold values from -6 to 6
- conv_in: bfloat16 [3, 3, 3, 32, 32], replicated, may hold values from -0.21875 to 0.21875
- conv_out: bfloat16 [3, 3, 3, 32, 32], replicated, may hold values from -0.21875 to 0.21875
- norm_gain: float32 [256], replicated, may hold values from 0.1 to 1.9
- q_weight: bfloat16 [256, 256], replicated, may hold values from -3 to 3
- kv_weight: bfloat16 [256, 512], replicated, may hold values from -0.375 to 0.375
- out_weight: bfloat16 [256, 256], replicated, may hold values from -0.375 to 0.375
- up_weight: bfloat16 [256, 256], replicated, may hold values from -0.375 to 0.375
Outputs:
- joined_out: bfloat16 [64, 256, 128, 32], P('gx', 'gy', 'gz')
The draws below stay inside these ranges and needn't reach their ends.
All inputs are finite; a program needn't handle non-finite values.
Results may differ from the reference program's by a relative error of at most 0.012.
The reference program's roundings to bfloat16 on the way (of `encoded`, `normed`, `attended`, `mixture` and `joined`) count: a program that leaves them out, or rounds other values in their place, can miss the bound.
Values may be sent and summed in bfloat16 or wider, within the bound.
A program may use at most 64 MiB of HBM per device.

```python
import math
import jax
import jax.numpy as jnp
from jax import lax

C = 32
HEADS = 8
F = 256
NX = 64
NY = 256
NZ = 128


def draw_q_weight(key, part):
    factor = 2.5
    values = jax.random.normal(key, (F, F), jnp.float32) * (factor / math.sqrt(F))
    return jnp.clip(values, -3.0, 3.0).astype(jnp.bfloat16)


def levels(stream_key, extent, cuts, smallest, top_value):
    factor_of = 1.0
    for dim, shards_of in cuts:
        steps = jax.random.uniform(jax.random.fold_in(jax.random.fold_in(stream_key, 6), dim), (shards_of,), jnp.float32, smallest / len(cuts), top_value / len(cuts))
        factor_of = factor_of * jnp.repeat(jnp.exp(steps), extent[dim] // shards_of).reshape((-1,) + (1,) * (len(extent) - 1 - dim))
    return factor_of


def scatter_about(own_key, shape, deviation, bound, pieces=(), held_as=jnp.bfloat16):
    entries = jax.random.normal(own_key, shape, jnp.float32) * deviation
    if len(pieces) > 0:
        entries = levels(own_key, shape, pieces, -0.22, 0.18) * entries
    return jnp.clip(entries, min=-bound, max=bound).astype(held_as)


def setup_inputs(seed: int = 0) -> dict:
    seeds = jax.random.split(jax.random.key(seed), 9)
    return {
        "volume": scatter_about(seeds[0], (NX, NY, NZ, C), 1.0, 6.0, ((0, 8), (1, 8), (2, 8))),
        "conv_in": scatter_about(seeds[1], (3, 3, 3, C, C), (27 * C) ** -0.5, 0.21875),
        "conv_out": scatter_about(seeds[2], (3, 3, 3, C, C), (27 * C) ** -0.5, 0.21875),
        "norm_gain": jnp.clip(1.0 + 0.18 * jax.random.normal(seeds[3], (F,), jnp.float32), 0.1, 1.9),
        "q_weight": draw_q_weight(jax.random.fold_in(seeds[8], 71), 0),
        "kv_weight": scatter_about(seeds[5], (F, 2 * F), F ** -0.5, 0.375),
        "out_weight": scatter_about(seeds[6], (F, F), F ** -0.5, 0.375),
        "up_weight": scatter_about(seeds[7], (F, F), F ** -0.5, 0.375),
    }


def convolve(volume_map, kernel):
    return lax.conv_general_dilated(volume_map[None], kernel, (1, 1, 1), 'SAME', dimension_numbers=('NDHWC', 'DHWIO', 'NDHWC'), preferred_element_type=jnp.float32)[0]

def tokenize(volume_map):
    extent_x, extent_y, extent_z, channels = volume_map.shape
    grid_cells = volume_map.reshape(extent_x // 8, 2, 4, extent_y // 8, 2, 4, extent_z // 8, 2, 4, channels).mean(axis=(2, 5, 8))
    grid_cells = grid_cells.transpose(0, 2, 4, 1, 3, 5, 6)
    return grid_cells.reshape(extent_x // 8 * (extent_y // 8) * (extent_z // 8), 8 * channels)

def spread_cells(token_rows, extent_x, extent_y, extent_z):
    channels = token_rows.shape[1] // 8
    grid_cells = token_rows.reshape(extent_x // 8, extent_y // 8, extent_z // 8, 2, 2, 2, channels).transpose(0, 3, 1, 4, 2, 5, 6)
    grid_cells = jnp.broadcast_to(grid_cells[:, :, None, :, :, None, :, :, None, :], (extent_x // 8, 2, 4, extent_y // 8, 2, 4, extent_z // 8, 2, 4, channels))
    return grid_cells.reshape(extent_x, extent_y, extent_z, channels)

def layer_norm(tokens, norm_gain):
    center = tokens - tokens.mean(axis=1, keepdims=True)
    spread = (center * center).mean(axis=1, keepdims=True)
    return (center * lax.rsqrt(spread + 1e-05) * norm_gain).astype(jnp.bfloat16)

def attention(queries, key_rows, value_rows):
    token_count = queries.shape[0]
    head_size = F // HEADS
    block_rows = math.gcd(token_count, 2048)

    def split_heads(matrix):
        return matrix.reshape(token_count, HEADS, head_size).transpose(1, 0, 2)

    def one_head(operands):
        head_query, head_keys, head_values = operands
        query_blocks = head_query.reshape(token_count // block_rows, block_rows, head_size)

        def one_block(query_block):
            scores = jnp.dot(query_block, head_keys.T, preferred_element_type=jnp.float32) * head_size ** (-0.5)
            row_peak = scores.max(axis=1, keepdims=True)
            weights = jnp.exp(scores - row_peak)
            numerator = jnp.dot(weights.astype(jnp.bfloat16), head_values, preferred_element_type=jnp.float32)
            return (numerator / weights.sum(axis=1, keepdims=True)).astype(jnp.bfloat16)
        return lax.map(one_block, query_blocks).reshape(token_count, head_size)
    result = lax.map(one_head, (split_heads(queries), split_heads(key_rows), split_heads(value_rows)))
    return result.transpose(1, 0, 2).reshape(token_count, F)

def reference(volume, conv_in, conv_out, norm_gain, q_weight, kv_weight, out_weight, up_weight):
    encoded = jax.nn.relu(convolve(volume, conv_in)).astype(jnp.bfloat16)
    tokens = tokenize(encoded.astype(jnp.float32))
    normed = layer_norm(tokens, norm_gain)
    queries = jnp.dot(normed, q_weight, preferred_element_type=jnp.float32).astype(jnp.bfloat16)
    key_value = jnp.dot(normed, kv_weight, preferred_element_type=jnp.float32).astype(jnp.bfloat16)
    attended = attention(queries, key_value[:, :F], key_value[:, F:])
    mixture = (tokens + jnp.dot(attended, out_weight, preferred_element_type=jnp.float32)).astype(jnp.bfloat16)
    upward = jnp.dot(mixture, up_weight, preferred_element_type=jnp.float32)
    joined = (encoded.astype(jnp.float32) + spread_cells(upward, NX, NY, NZ)).astype(jnp.bfloat16)
    return convolve(joined, conv_out).astype(jnp.bfloat16)
```

```python
import functools

import jax
import jax.numpy as jnp
from jax import lax
from jax.experimental import pallas as pl
from jax.experimental.pallas import tpu as pltpu
from jax.sharding import PartitionSpec as P

BF = jnp.bfloat16
F32 = jnp.float32
MESH = pl.DeviceIdType.MESH
STEPS = [(a, b, c) for a in (-1, 0, 1) for b in (-1, 0, 1) for c in (-1, 0, 1) if (a, b, c) != (0, 0, 0)]


def iota(shape, dim):
    return lax.broadcasted_iota(jnp.int32, shape, dim)


def dot(left, right):
    return jnp.dot(left, right, preferred_element_type=F32)


def roll(value, shift, axis):
    return pltpu.roll(value, shift, axis)


def lane_window(c, width):
    if c == 0:
        return (0, 512), (128, 512)
    if c == 1:
        return (384, 128), (0, 128)
    return (0, 128), (640, 128)


def kernel(sizes, x_hbm, win_hbm, wout_hbm, gain_hbm, qw_hbm, kvw_hbm, ow_hbm, uw_hbm, out_ref,
           vol, vol_lo, vol_hi, enc, enc_lo, enc_hi, joi, joi_lo, joi_hi, rows_v, rows_e,
           win, wout, gain, qw, kvw, ow, uw, taps, lhs, acc, tokens_s,
           qbuf, kvbuf, kmask, vmask, osend, orecv, lsend, lrecv, up, uppad,
           load_sem, vs, vr, es, er, us, ur, gs, gr, rs, rr):
    GX, GY, GZ = sizes
    gx, gy, gz = lax.axis_index("gx"), lax.axis_index("gy"), lax.axis_index("gz")
    n_row, n_col = (GY // 2) * GZ, GX * 2

    def at_mesh(x, y, z):
        return (x, y, z)

    def row_peer(i, sign=1):
        return at_mesh(gx, (gy + GY + sign * 2 * (i // GZ)) % GY, (gz + GZ + sign * (i % GZ)) % GZ)

    def col_peer(i):
        return at_mesh((gx + i // 2) % GX, gy // 2 * 2 + (gy + i % 2) % 2, gz)

    def inside(a, b, c):
        ok = None
        for at, step, size in ((gx, a, GX), (gy, b, GY), (gz, c, GZ)):
            if step:
                here = at < size - 1 if step > 0 else at > 0
                ok = here if ok is None else ok & here
        return ok

    def neighbour(a, b, c):
        return at_mesh(gx + a, gy + b, gz + c)

    for ref in (vol, enc, vol_lo, vol_hi, enc_lo, enc_hi, uppad):
        ref[...] = jnp.zeros(ref.shape, ref.dtype)
    barrier = pltpu.get_barrier_semaphore()
    for step in STEPS:
        @pl.when(inside(*step))
        def _(step=step):
            pl.semaphore_signal(barrier, inc=1, device_id=neighbour(*step), device_id_type=MESH)
    for i in range(1, n_row):
        pl.semaphore_signal(barrier, inc=1, device_id=row_peer(i), device_id_type=MESH)
    for i in range(1, n_col):
        pl.semaphore_signal(barrier, inc=1, device_id=col_peer(i), device_id_type=MESH)

    own = (pl.ds(1, 8), pl.ds(0, 32), pl.ds(128, 512))
    loads = [pltpu.make_async_copy(x_hbm, vol.at[own], load_sem.at[0])]
    pairs = [(win_hbm, win), (wout_hbm, wout), (gain_hbm, gain), (qw_hbm, qw), (kvw_hbm, kvw), (ow_hbm, ow), (uw_hbm, uw)]
    loads += [pltpu.make_async_copy(s, d, load_sem.at[i + 1]) for i, (s, d) in enumerate(pairs)]
    for copy in loads:
        copy.start()

    def pack_rows(main, rows):
        r, k = iota((32, 256), 0), iota((32, 256), 1)
        wanted = jnp.where(r < 16, r * 32, (r - 16) * 32 + 31)
        picked = dot((wanted == k).astype(F32).astype(BF), main[own].reshape(256, 512))
        rows[...] = picked.astype(BF).reshape(2, 16, 512)

    def remote(src, dst, send, recv, step):
        copy = pltpu.make_async_remote_copy(src_ref=src, dst_ref=dst, send_sem=send, recv_sem=recv,
                                            device_id=neighbour(*step), device_id_type=MESH)
        return copy, pltpu.make_async_copy(dst, dst, recv), pltpu.make_async_copy(src, src, send)

    def halo_copies(main, rows, lo, hi, send, recv):
        copies = []
        for n, (a, b, c) in enumerate(STEPS):
            (s0, width), (d0, _) = lane_window(c, 512)
            if b == 0:
                sx = {-1: pl.ds(1, 1), 0: pl.ds(1, 8), 1: pl.ds(8, 1)}[a]
                dx = {-1: pl.ds(9, 1), 0: pl.ds(1, 8), 1: pl.ds(0, 1)}[a]
                src = main.at[sx, pl.ds(0, 32), pl.ds(128 + s0, width)]
                dst = main.at[dx, pl.ds(0, 32), pl.ds(d0, width)]
            else:
                src = rows.at[1 if b == 1 else 0, pl.ds(0, 16), pl.ds(s0, width)]
                dst = (lo if b == 1 else hi).at[1 - a, pl.ds(0, 16), pl.ds(d0, width)]
            copies.append(remote(src, dst, send.at[n], recv.at[n], (a, b, c)))
        return copies

    def start_all(copies):
        for step, (copy, _, _) in zip(STEPS, copies):
            @pl.when(inside(*step))
            def _(copy=copy):
                copy.start()

    def arrived(copies):
        for (a, b, c), (_, landing, _) in zip(STEPS, copies):
            @pl.when(inside(-a, -b, -c))
            def _(landing=landing):
                landing.wait()

    def departed(copies):
        for step, (_, _, leaving) in zip(STEPS, copies):
            @pl.when(inside(*step))
            def _(leaving=leaving):
                leaving.wait()

    def spread_taps(w):
        k, n = iota((32, 512), 0), iota((32, 512), 1)
        place = ((n % 32 == k) & (n // 128 == (n % 128) // 32)).astype(F32).astype(BF)
        moved = dot(w[...], place).astype(BF)
        taps[...] = jnp.zeros(taps.shape, BF)
        for dx in range(3):
            for dy in range(3):
                first = (dx * 3 + dy) * 96
                for m in range(2):
                    for block in range(6):
                        total = None
                        for g in range(4):
                            dz = block - g
                            if 0 <= dz <= 2:
                                piece = moved[first + dz * 32:first + dz * 32 + 32, g * 128:g * 128 + 128]
                                total = piece if total is None else total + piece
                        r0 = dx * 512 + (4 * m + 3 + block) * 32
                        taps[dy, r0:r0 + 32, m * 128:m * 128 + 128] = total

    def convolve(main, lo, hi, emit):
        row8 = iota((8, 768), 0)

        def three(rim):
            before, here, after = (rim[i].astype(F32)[0:8] for i in range(3))
            return (jnp.where(row8 == 0, roll(before, 1, 0), roll(here, 1, 0)), here,
                    jnp.where(row8 == 7, roll(after, 7, 0), roll(here, 7, 0)))

        rims = [jnp.concatenate(p, axis=0).astype(BF) for p in zip(three(lo), three(hi))]
        for dx in range(3):
            for h in range(2):
                lhs[h * 256:h * 256 + 256, dx * 512:dx * 512 + 512] = main[dx:dx + 8, :, h * 256:h * 256 + 512].reshape(256, 512)
                lhs[512 + 16 * h:528 + 16 * h, dx * 512:dx * 512 + 512] = rims[dx][:, h * 256:h * 256 + 512]

        def one(dy, carry):
            acc[dy, 0:544, :] = dot(lhs[...], taps[dy])
            return carry

        lax.fori_loop(0, 3, one, 0)
        row = iota((32, 256), 0)

        def join(x, carry):
            for h in range(2):
                at = pl.ds(pl.multiple_of(h * 256 + x * 32, 32), 32)
                below = jnp.where(row == 0, acc[0, pl.ds(512 + 16 * h + x, 1), :], roll(acc[0, at, :], 1, 0))
                above = jnp.where(row == 31, acc[2, pl.ds(520 + 16 * h + x, 1), :], roll(acc[2, at, :], 31, 0))
                emit(x, h, below + acc[1, at, :] + above)
            return carry

        lax.fori_loop(0, 8, join, 0)

    loads[0].wait()
    pack_rows(vol, rows_v)
    neighbours = (1 + (gx > 0).astype(jnp.int32) + (gx < GX - 1).astype(jnp.int32))
    neighbours *= (1 + (gy > 0).astype(jnp.int32) + (gy < GY - 1).astype(jnp.int32))
    neighbours *= (1 + (gz > 0).astype(jnp.int32) + (gz < GZ - 1).astype(jnp.int32))
    pl.semaphore_wait(barrier, neighbours - 1 + n_row - 1 + n_col - 1)
    vol_copies = halo_copies(vol, rows_v, vol_lo, vol_hi, vs, vr)
    start_all(vol_copies)
    for copy in loads[1:]:
        copy.wait()
    spread_taps(win)
    arrived(vol_copies)

    def keep_encoded(x, h, value):
        enc[1 + x, :, 128 + 256 * h:384 + 256 * h] = jnp.maximum(value, 0.0).astype(BF)

    convolve(vol, vol_lo, vol_hi, keep_encoded)

    r, k = iota((32, 256), 0), iota((32, 256), 1)
    pool = ((k // 128 == r // 16) & ((k % 32) // 4 == 2 * (r % 4) + (r // 8) % 2)).astype(F32).astype(BF)
    sums = dot(pool, enc[own].reshape(256, 512))
    row8, group8 = iota((8, 128), 0), iota((8, 128), 1) // 32
    chunks = []
    for q in range(4):
        part = sums[:, q * 128:q * 128 + 128]
        part = part + roll(part, 64, 1)
        chunks.append(part + roll(part, 32, 1))

    def cell(ab, c):
        return jnp.where(row8 < 4, chunks[c][ab * 8:ab * 8 + 8], chunks[2 + c][ab * 8:ab * 8 + 8])

    sides = []
    for a in range(2):
        side = cell(2 * a + 1, 1)
        for n, (b, c) in enumerate(((0, 0), (0, 1), (1, 0))):
            side = jnp.where(group8 == n, cell(2 * a + b, c), side)
        sides.append(side)
    tokens = jnp.concatenate(sides, axis=1) * (1.0 / 64.0)
    tokens_s[...] = tokens
    center = tokens - jnp.mean(tokens, axis=1, keepdims=True)
    variance = jnp.mean(center * center, axis=1, keepdims=True)
    normed = center * lax.rsqrt(variance + 1e-05) * gain[...]
    normed = jnp.concatenate([normed, jnp.zeros_like(normed)], axis=0).astype(BF)
    queries = dot(normed, qw[...])[0:8]
    key_value = dot(normed, kvw[...])[0:8]
    qbuf[0] = jnp.concatenate([queries[:, i * 128:i * 128 + 128] for i in range(2)], axis=0).astype(BF)
    kvbuf[0] = jnp.concatenate([key_value[:, i * 128:i * 128 + 128] for i in range(4)], axis=0).astype(BF)

    q_all = pltpu.make_async_copy(qbuf.at[pl.ds(1, n_row - 1)], qbuf.at[pl.ds(1, n_row - 1)], gr.at[0])
    kv_all = pltpu.make_async_copy(kvbuf.at[pl.ds(1, n_col - 1)], kvbuf.at[pl.ds(1, n_col - 1)], gr.at[1])
    q_gone = pltpu.make_async_copy(qbuf.at[pl.ds(1, n_row - 1)], qbuf.at[pl.ds(1, n_row - 1)], gs.at[0])
    kv_gone = pltpu.make_async_copy(kvbuf.at[pl.ds(1, n_col - 1)], kvbuf.at[pl.ds(1, n_col - 1)], gs.at[1])
    for i in range(n_row - 1, 0, -1):
        pltpu.make_async_remote_copy(src_ref=qbuf.at[0], dst_ref=qbuf.at[i], send_sem=gs.at[0], recv_sem=gr.at[0],
                                     device_id=row_peer(i), device_id_type=MESH).start()
    for i in range(n_col - 1, 0, -1):
        pltpu.make_async_remote_copy(src_ref=kvbuf.at[0], dst_ref=kvbuf.at[i], send_sem=gs.at[1], recv_sem=gr.at[1],
                                     device_id=col_peer(i), device_id_type=MESH).start()
    pack_rows(enc, rows_e)
    enc_copies = halo_copies(enc, rows_e, enc_lo, enc_hi, es, er)
    start_all(enc_copies)
    spread_taps(wout)

    q_all.wait()
    kv_all.wait()
    n_keys = n_col * 16
    lane_group = iota((n_keys, 128), 1) // 32
    keys = kvbuf[:, 0:16, :].reshape(n_keys, 128)
    values = kvbuf[:, 16:32, :].reshape(n_keys, 128)
    for g in range(4):
        mine = (lane_group == g).astype(F32).astype(BF)
        kmask[g] = keys * mine
        vmask[g, :, 0:128] = values * mine
        vmask[g, :, 128:256] = mine
    slots = min(8, n_row)
    n_rows = slots * 16
    same_half = (iota((n_rows, n_keys), 0) // 8) % 2 == (iota((n_rows, n_keys), 1) // 8) % 2
    group = iota((n_rows, 128), 1) // 32
    compact = iota((slots, 16, 128), 1) == iota((slots, 16, 128), 2) % 32

    def attend(i, carry):
        at = pl.ds(i * slots, slots)
        query = qbuf[at].reshape(n_rows, 128)
        total, peaks = jnp.zeros((n_rows, 256), F32), jnp.zeros((n_rows, 128), F32)
        for g in range(4):
            scores = lax.dot_general(query, kmask[g], (((1,), (1,)), ((), ())), preferred_element_type=F32)
            scores = jnp.where(same_half, scores * 32 ** (-0.5), -1e30)
            peak = jnp.max(scores, axis=1, keepdims=True)
            total = total + dot(jnp.exp(scores - peak).astype(BF), vmask[g])
            peaks = jnp.where(group == g, peak, peaks)
        weight = total[:, 128:256]
        osend[at] = (total[:, 0:128] / weight).astype(BF).reshape(slots, 16, 128)
        level = (peaks + jnp.log(weight)).reshape(slots, 16, 128)
        lsend[at] = jnp.sum(jnp.where(compact, level, 0.0), axis=1, keepdims=True)
        return carry

    lax.fori_loop(0, n_row // slots, attend, 0)
    others = pl.ds(1, n_row - 1)
    for i in range(n_row - 1, 0, -1):
        pltpu.make_async_remote_copy(src_ref=lsend.at[i], dst_ref=lrecv.at[i], send_sem=rs.at[1], recv_sem=rr.at[1],
                                     device_id=row_peer(i, -1), device_id_type=MESH).start()
        pltpu.make_async_remote_copy(src_ref=osend.at[i], dst_ref=orecv.at[i], send_sem=rs.at[0], recv_sem=rr.at[0],
                                     device_id=row_peer(i, -1), device_id_type=MESH).start()
    orecv[0] = osend[0]
    lrecv[0] = lsend[0]
    arrived(enc_copies)
    pltpu.make_async_copy(orecv.at[others], orecv.at[others], rr.at[0]).wait()
    pltpu.make_async_copy(lrecv.at[others], lrecv.at[others], rr.at[1]).wait()

    levels = lrecv[...]
    share = jnp.exp(levels - jnp.max(levels, axis=0, keepdims=True))
    share = share / jnp.sum(share, axis=0, keepdims=True)
    spot = iota((n_row, 16, 128), 1) == iota((n_row, 16, 128), 2) % 32
    share = jnp.where(spot, share, 0.0).reshape(n_row * 16, 128)
    high = share.astype(BF)
    low = (share - high.astype(F32)).astype(BF)
    blocks = ((iota((256, 128), 0) % 128) // 32 == iota((256, 128), 1) // 32).astype(F32).astype(BF)
    share = dot(jnp.concatenate([high, low], axis=1), blocks).reshape(n_row, 16, 128)
    attended = jnp.sum(share * orecv[...].astype(F32), axis=0)
    attended = jnp.concatenate([attended[0:8], attended[8:16]], axis=1)
    attended = jnp.concatenate([attended, jnp.zeros_like(attended)], axis=0).astype(BF)
    mixture = tokens_s[...] + dot(attended, ow[...])[0:8]
    mixture = jnp.concatenate([mixture, jnp.zeros_like(mixture)], axis=0).astype(BF)
    r, k = iota((16, 16), 0), iota((16, 16), 1)
    twice = ((r // 8) * 4 + (r % 8) // 2 == k).astype(F32).astype(BF)
    upward = dot(dot(twice, mixture).astype(BF), uw[...])
    odd, right = row8 % 2 == 1, group8 >= 2
    for a in range(2):
        first = upward[0:8, a * 128:a * 128 + 128]
        second = upward[8:16, a * 128:a * 128 + 128]
        plane = jnp.where(right, jnp.where(odd, second, roll(second, 64, 1)), jnp.where(odd, roll(first, 64, 1), first))
        for y in range(8):
            up[a, y, 0] = plane[y:y + 1, :]
            uppad[1 + a, 1 + y, 1] = plane[y:y + 1, :]

    up_copies = []
    for n, (a, b, c) in enumerate(STEPS):
        sx = {-1: pl.ds(0, 1), 0: pl.ds(0, 2), 1: pl.ds(1, 1)}[a]
        dx = {-1: pl.ds(3, 1), 0: pl.ds(1, 2), 1: pl.ds(0, 1)}[a]
        sy = {-1: pl.ds(0, 1), 0: pl.ds(0, 8), 1: pl.ds(7, 1)}[b]
        dy = {-1: pl.ds(9, 1), 0: pl.ds(1, 8), 1: pl.ds(0, 1)}[b]
        up_copies.append(remote(up.at[sx, sy, pl.ds(0, 1)], uppad.at[dx, dy, pl.ds(1 - c, 1)], us.at[n], ur.at[n], (a, b, c)))
    start_all(up_copies)
    arrived(up_copies)

    group1 = iota((1, 128), 1) // 32

    def wide(plane, y):
        middle = uppad[plane, y, 1]
        parts = [uppad[plane, y, 0]]
        for q in range(4):
            part = jnp.where(group1 == q, middle, 0.0)
            part = part + roll(part, 64, 1)
            parts.append(part + roll(part, 32, 1))
        return jnp.concatenate(parts + [uppad[plane, y, 2]], axis=1)

    row_wide = iota((8, 768), 0)
    for plane in range(4):
        xs = (range(0, 1), range(1, 5), range(5, 9), range(9, 10))[plane]
        for y2 in range(2):
            four = [wide(plane, 1 + 4 * y2 + i) for i in range(4)]
            more = jnp.concatenate([jnp.where(row_wide < 4, four[2 * i], four[2 * i + 1]) for i in range(2)], axis=0)
            for x in xs:
                joi[x, 16 * y2:16 * y2 + 16, :] = (enc[x, 16 * y2:16 * y2 + 16, :].astype(F32) + more).astype(BF)
    row_rim = iota((16, 768), 0)
    for rim, full, y in ((enc_lo, joi_lo, 0), (enc_hi, joi_hi, 9)):
        planes = [wide(plane, y) for plane in range(4)]
        full[0] = (rim[0].astype(F32) + planes[0]).astype(BF)
        full[1] = (rim[1].astype(F32) + jnp.where(row_rim < 4, planes[1], planes[2])).astype(BF)
        full[2] = (rim[2].astype(F32) + planes[3]).astype(BF)

    def keep_result(x, h, value):
        out_ref[x, :, 256 * h:256 * h + 256] = value.astype(BF)

    convolve(joi, joi_lo, joi_hi, keep_result)

    departed(vol_copies)
    departed(enc_copies)
    departed(up_copies)
    q_gone.wait()
    kv_gone.wait()
    pltpu.make_async_copy(orecv.at[others], orecv.at[others], rs.at[0]).wait()
    pltpu.make_async_copy(lrecv.at[others], lrecv.at[others], rs.at[1]).wait()


def on_device(sizes, volume, conv_in, conv_out, norm_gain, q_weight, kv_weight, out_weight, up_weight):
    n_row, n_col = (sizes[1] // 2) * sizes[2], sizes[0] * 2
    wide = volume.reshape(8, 32, 512)
    padded, rim, rows = (10, 32, 768), (3, 16, 768), (2, 16, 512)
    vmem = pltpu.VMEM
    scratch = [vmem(padded, BF), vmem(rim, BF), vmem(rim, BF)] * 3 + [vmem(rows, BF)] * 2
    scratch += [vmem((864, 32), BF)] * 2 + [vmem((1, 256), F32), vmem((256, 256), BF), vmem((256, 512), BF), vmem((256, 256), BF), vmem((256, 256), BF)]
    scratch += [vmem((3, 1536, 256), BF), vmem((544, 1536), BF), vmem((3, 552, 256), F32), vmem((8, 256), F32)]
    scratch += [vmem((n_row, 16, 128), BF), vmem((n_col, 32, 128), BF), vmem((4, n_col * 16, 128), BF), vmem((4, n_col * 16, 256), BF)]
    scratch += [vmem((n_row, 16, 128), BF)] * 2 + [vmem((n_row, 1, 128), F32)] * 2
    scratch += [vmem((2, 8, 1, 1, 128), F32), vmem((4, 10, 3, 1, 128), F32)]
    dma = pltpu.SemaphoreType.DMA
    scratch += [dma((8,))] + [dma((26,))] * 6 + [dma((2,))] * 4
    result = pl.pallas_call(
        functools.partial(kernel, sizes),
        out_shape=jax.ShapeDtypeStruct((8, 32, 512), BF),
        in_specs=[pl.BlockSpec(memory_space=pl.ANY)] * 8,
        out_specs=pl.BlockSpec(memory_space=pltpu.VMEM),
        scratch_shapes=scratch,
        compiler_params=pltpu.CompilerParams(collective_id=0, has_side_effects=True, vmem_limit_bytes=48 * 2**20),
    )(wide, conv_in.reshape(864, 32), conv_out.reshape(864, 32), norm_gain.reshape(1, 256), q_weight, kv_weight, out_weight, up_weight)
    return result.reshape(8, 32, 16, 32)


def solution(mesh):
    placed = (P("gx", "gy", "gz", None), P(), P(), P(), P(), P(), P(), P())
    sizes = tuple(mesh.shape[name] for name in ("gx", "gy", "gz"))
    return jax.shard_map(
        functools.partial(on_device, sizes), mesh=mesh, in_specs=placed, out_specs=P("gx", "gy", "gz", None), check_vma=False
    )
```

```python
import functools

import jax
import jax.numpy as jnp
from jax import lax
from jax.experimental import pallas as pl
from jax.experimental.pallas import tpu as pltpu
from jax.sharding import PartitionSpec as P

BF = jnp.bfloat16
F32 = jnp.float32
MESH = pl.DeviceIdType.MESH
STEPS = [(a, b, c) for a in (-1, 0, 1) for b in (-1, 0, 1) for c in (-1, 0, 1) if (a, b, c) != (0, 0, 0)]
STEPS.sort(key=lambda step: -sum(abs(v) for v in step))


def iota(shape, dim):
    return lax.broadcasted_iota(jnp.int32, shape, dim)


def dot(left, right):
    return jnp.dot(left, right, preferred_element_type=F32)


def roll(value, shift, axis):
    return pltpu.roll(value, shift, axis)


def lane_window(c, width):
    if c == 0:
        return (0, 512), (128, 512)
    if c == 1:
        return (384, 128), (0, 128)
    return (0, 128), (640, 128)


def kernel(sizes, x_hbm, win_hbm, wout_hbm, gain_hbm, qw_hbm, kvw_hbm, ow_hbm, uw_hbm, out_ref,
           raw, vol, vol_lo, vol_hi, enc, enc_lo, enc_hi, joi, joi_lo, joi_hi, rows_v, rows_e,
           win, wout, gain, qw, kvw, ow, uw, taps, lhs, acc, tokens_s,
           qbuf, kvbuf, kmask, vmask, osend, orecv, lsend, lrecv, up, uppad,
           load_sem, vs, vr, es, er, us, ur, gs, gr, rs, rr):
    GX, GY, GZ = sizes
    gx, gy, gz = lax.axis_index("gx"), lax.axis_index("gy"), lax.axis_index("gz")
    n_row, n_col = (GY // 2) * GZ, GX * 2

    def at_mesh(x, y, z):
        return (x, y, z)

    def row_peer(i, sign=1):
        return at_mesh(gx, (gy + GY + sign * 2 * (i // GZ)) % GY, (gz + GZ + sign * (i % GZ)) % GZ)

    def col_peer(i):
        return at_mesh((gx + i // 2) % GX, gy // 2 * 2 + (gy + i % 2) % 2, gz)

    row_far = sorted(range(1, n_row), key=lambda i: -2 * min(i // GZ, GY // 2 - i // GZ) - min(i % GZ // 2, GZ // 2 - i % GZ // 2) - i % 2)
    col_far = sorted(range(1, n_col), key=lambda i: -min(i // 2, GX - i // 2))

    def inside(a, b, c):
        ok = None
        for at, step, size in ((gx, a, GX), (gy, b, GY), (gz, c, GZ)):
            if step:
                here = at < size - 1 if step > 0 else at > 0
                ok = here if ok is None else ok & here
        return ok

    def neighbour(a, b, c):
        return at_mesh(gx + a, gy + b, gz + c)

    for ref in (vol, enc):
        for x in (0, 9):
            ref[x] = jnp.zeros((32, 768), BF)
        for z in (0, 640):
            ref[1:9, :, z:z + 128] = jnp.zeros((8, 32, 128), BF)
    for ref in (vol_lo, vol_hi, enc_lo, enc_hi, uppad):
        ref[...] = jnp.zeros(ref.shape, ref.dtype)
    barrier = pltpu.get_barrier_semaphore()
    for step in STEPS:
        @pl.when(inside(*step))
        def _(step=step):
            pl.semaphore_signal(barrier, inc=1, device_id=neighbour(*step), device_id_type=MESH)
    for i in range(1, n_row):
        pl.semaphore_signal(barrier, inc=1, device_id=row_peer(i), device_id_type=MESH)
    for i in range(1, n_col):
        pl.semaphore_signal(barrier, inc=1, device_id=col_peer(i), device_id_type=MESH)

    own = (pl.ds(1, 8), pl.ds(0, 32), pl.ds(128, 512))
    loads = [pltpu.make_async_copy(x_hbm, raw, load_sem.at[0])]
    pairs = [(win_hbm, win), (wout_hbm, wout), (gain_hbm, gain), (qw_hbm, qw), (kvw_hbm, kvw), (ow_hbm, ow), (uw_hbm, uw)]
    loads += [pltpu.make_async_copy(s, d, load_sem.at[i + 1]) for i, (s, d) in enumerate(pairs)]
    for copy in loads:
        copy.start()

    def pack_rows(main, rows):
        r, k = iota((32, 256), 0), iota((32, 256), 1)
        wanted = jnp.where(r < 16, r * 32, (r - 16) * 32 + 31)
        picked = dot((wanted == k).astype(F32).astype(BF), main[own].reshape(256, 512))
        rows[...] = picked.astype(BF).reshape(2, 16, 512)

    def remote(src, dst, send, recv, step):
        copy = pltpu.make_async_remote_copy(src_ref=src, dst_ref=dst, send_sem=send, recv_sem=recv,
                                            device_id=neighbour(*step), device_id_type=MESH)
        return copy, pltpu.make_async_copy(dst, dst, recv), pltpu.make_async_copy(src, src, send)

    def halo_copies(main, rows, lo, hi, send, recv):
        copies = []
        for n, (a, b, c) in enumerate(STEPS):
            (s0, width), (d0, _) = lane_window(c, 512)
            if b == 0:
                sx = {-1: pl.ds(1, 1), 0: pl.ds(1, 8), 1: pl.ds(8, 1)}[a]
                dx = {-1: pl.ds(9, 1), 0: pl.ds(1, 8), 1: pl.ds(0, 1)}[a]
                src = main.at[sx, pl.ds(0, 32), pl.ds(128 + s0, width)]
                dst = main.at[dx, pl.ds(0, 32), pl.ds(d0, width)]
            else:
                src = rows.at[1 if b == 1 else 0, pl.ds(0, 16), pl.ds(s0, width)]
                dst = (lo if b == 1 else hi).at[1 - a, pl.ds(0, 16), pl.ds(d0, width)]
            copies.append(remote(src, dst, send.at[n], recv.at[n], (a, b, c)))
        return copies

    def start_all(copies):
        for step, (copy, _, _) in zip(STEPS, copies):
            @pl.when(inside(*step))
            def _(copy=copy):
                copy.start()

    def arrived(copies):
        for (a, b, c), (_, landing, _) in zip(STEPS, copies):
            @pl.when(inside(-a, -b, -c))
            def _(landing=landing):
                landing.wait()

    def departed(copies):
        for step, (_, _, leaving) in zip(STEPS, copies):
            @pl.when(inside(*step))
            def _(leaving=leaving):
                leaving.wait()

    def spread_taps(w):
        k, n = iota((32, 512), 0), iota((32, 512), 1)
        place = ((n % 32 == k) & (n // 128 == (n % 128) // 32)).astype(F32).astype(BF)
        moved = dot(w[...], place).astype(BF)
        taps[...] = jnp.zeros(taps.shape, BF)
        for dx in range(3):
            for dy in range(3):
                first = (dx * 3 + dy) * 96
                for m in range(2):
                    for block in range(6):
                        total = None
                        for g in range(4):
                            dz = block - g
                            if 0 <= dz <= 2:
                                piece = moved[first + dz * 32:first + dz * 32 + 32, g * 128:g * 128 + 128]
                                total = piece if total is None else total + piece
                        r0 = dx * 512 + (4 * m + 3 + block) * 32
                        taps[dy, r0:r0 + 32, m * 128:m * 128 + 128] = total

    def convolve(main, lo, hi, emit):
        row8 = iota((8, 768), 0)

        def three(rim):
            before, here, after = (rim[i].astype(F32)[0:8] for i in range(3))
            return (jnp.where(row8 == 0, roll(before, 1, 0), roll(here, 1, 0)), here,
                    jnp.where(row8 == 7, roll(after, 7, 0), roll(here, 7, 0)))

        rims = [jnp.concatenate(p, axis=0).astype(BF) for p in zip(three(lo), three(hi))]
        for dx in range(3):
            for h in range(2):
                lhs[h * 256:h * 256 + 256, dx * 512:dx * 512 + 512] = main[dx:dx + 8, :, h * 256:h * 256 + 512].reshape(256, 512)
                lhs[512 + 16 * h:528 + 16 * h, dx * 512:dx * 512 + 512] = rims[dx][:, h * 256:h * 256 + 512]

        def one(dy, carry):
            acc[dy, 0:544, :] = dot(lhs[...], taps[dy])
            return carry

        lax.fori_loop(0, 3, one, 0)
        row = iota((32, 256), 0)

        def join(x, carry):
            for h in range(2):
                at = pl.ds(pl.multiple_of(h * 256 + x * 32, 32), 32)
                below = jnp.where(row == 0, acc[0, pl.ds(512 + 16 * h + x, 1), :], roll(acc[0, at, :], 1, 0))
                above = jnp.where(row == 31, acc[2, pl.ds(520 + 16 * h + x, 1), :], roll(acc[2, at, :], 31, 0))
                emit(x, h, below + acc[1, at, :] + above)
            return carry

        lax.fori_loop(0, 8, join, 0)

    loads[0].wait()
    for x in range(8):
        vol[1 + x, :, 128:640] = raw[x].reshape(32, 512)
    pack_rows(vol, rows_v)
    neighbours = (1 + (gx > 0).astype(jnp.int32) + (gx < GX - 1).astype(jnp.int32))
    neighbours *= (1 + (gy > 0).astype(jnp.int32) + (gy < GY - 1).astype(jnp.int32))
    neighbours *= (1 + (gz > 0).astype(jnp.int32) + (gz < GZ - 1).astype(jnp.int32))
    pl.semaphore_wait(barrier, neighbours - 1 + n_row - 1 + n_col - 1)
    vol_copies = halo_copies(vol, rows_v, vol_lo, vol_hi, vs, vr)
    start_all(vol_copies)
    for copy in loads[1:]:
        copy.wait()
    spread_taps(win)
    arrived(vol_copies)

    def keep_encoded(x, h, value):
        enc[1 + x, :, 128 + 256 * h:384 + 256 * h] = jnp.maximum(value, 0.0).astype(BF)

    convolve(vol, vol_lo, vol_hi, keep_encoded)

    r, k = iota((32, 256), 0), iota((32, 256), 1)
    pool = ((k // 128 == r // 16) & ((k % 32) // 4 == 2 * (r % 4) + (r // 8) % 2)).astype(F32).astype(BF)
    sums = dot(pool, enc[own].reshape(256, 512))
    row8, group8 = iota((8, 128), 0), iota((8, 128), 1) // 32
    chunks = []
    for q in range(4):
        part = sums[:, q * 128:q * 128 + 128]
        part = part + roll(part, 64, 1)
        chunks.append(part + roll(part, 32, 1))

    def cell(ab, c):
        return jnp.where(row8 < 4, chunks[c][ab * 8:ab * 8 + 8], chunks[2 + c][ab * 8:ab * 8 + 8])

    sides = []
    for a in range(2):
        side = cell(2 * a + 1, 1)
        for n, (b, c) in enumerate(((0, 0), (0, 1), (1, 0))):
            side = jnp.where(group8 == n, cell(2 * a + b, c), side)
        sides.append(side)
    tokens = jnp.concatenate(sides, axis=1) * (1.0 / 64.0)
    tokens_s[...] = tokens
    center = tokens - jnp.mean(tokens, axis=1, keepdims=True)
    variance = jnp.mean(center * center, axis=1, keepdims=True)
    normed = center * lax.rsqrt(variance + 1e-05) * gain[...]
    normed = jnp.concatenate([normed, jnp.zeros_like(normed)], axis=0).astype(BF)
    queries = dot(normed, qw[...])[0:8]
    key_value = dot(normed, kvw[...])[0:8]
    qbuf[0] = jnp.concatenate([queries[:, i * 128:i * 128 + 128] for i in range(2)], axis=0).astype(BF)
    kvbuf[0] = jnp.concatenate([key_value[:, i * 128:i * 128 + 128] for i in range(4)], axis=0).astype(BF)

    q_all = pltpu.make_async_copy(qbuf.at[pl.ds(1, n_row - 1)], qbuf.at[pl.ds(1, n_row - 1)], gr.at[0])
    kv_all = pltpu.make_async_copy(kvbuf.at[pl.ds(1, n_col - 1)], kvbuf.at[pl.ds(1, n_col - 1)], gr.at[1])
    q_gone = pltpu.make_async_copy(qbuf.at[pl.ds(1, n_row - 1)], qbuf.at[pl.ds(1, n_row - 1)], gs.at[0])
    kv_gone = pltpu.make_async_copy(kvbuf.at[pl.ds(1, n_col - 1)], kvbuf.at[pl.ds(1, n_col - 1)], gs.at[1])
    for i in row_far:
        pltpu.make_async_remote_copy(src_ref=qbuf.at[0], dst_ref=qbuf.at[i], send_sem=gs.at[0], recv_sem=gr.at[0],
                                     device_id=row_peer(i), device_id_type=MESH).start()
    for i in col_far:
        pltpu.make_async_remote_copy(src_ref=kvbuf.at[0], dst_ref=kvbuf.at[i], send_sem=gs.at[1], recv_sem=gr.at[1],
                                     device_id=col_peer(i), device_id_type=MESH).start()
    pack_rows(enc, rows_e)
    enc_copies = halo_copies(enc, rows_e, enc_lo, enc_hi, es, er)
    start_all(enc_copies)
    spread_taps(wout)

    q_all.wait()
    kv_all.wait()
    n_keys = n_col * 16
    lane_group = iota((n_keys, 128), 1) // 32
    keys = kvbuf[:, 0:16, :].reshape(n_keys, 128)
    values = kvbuf[:, 16:32, :].reshape(n_keys, 128)
    for g in range(4):
        mine = (lane_group == g).astype(F32).astype(BF)
        kmask[g] = keys * mine
        vmask[g, :, 0:128] = values * mine
        vmask[g, :, 128:256] = mine
    slots = min(8, n_row)
    n_rows = slots * 16
    same_half = (iota((n_rows, n_keys), 0) // 8) % 2 == (iota((n_rows, n_keys), 1) // 8) % 2
    group = iota((n_rows, 128), 1) // 32
    compact = iota((slots, 16, 128), 1) == iota((slots, 16, 128), 2) % 32

    def attend(i, carry):
        at = pl.ds(i * slots, slots)
        query = qbuf[at].reshape(n_rows, 128)
        total, peaks = jnp.zeros((n_rows, 256), F32), jnp.zeros((n_rows, 128), F32)
        for g in range(4):
            scores = lax.dot_general(query, kmask[g], (((1,), (1,)), ((), ())), preferred_element_type=F32)
            scores = jnp.where(same_half, scores * 32 ** (-0.5), -1e30)
            peak = jnp.max(scores, axis=1, keepdims=True)
            total = total + dot(jnp.exp(scores - peak).astype(BF), vmask[g])
            peaks = jnp.where(group == g, peak, peaks)
        weight = total[:, 128:256]
        osend[at] = (total[:, 0:128] / weight).astype(BF).reshape(slots, 16, 128)
        level = (peaks + jnp.log(weight)).reshape(slots, 16, 128)
        lsend[at] = jnp.sum(jnp.where(compact, level, 0.0), axis=1, keepdims=True)
        return carry

    lax.fori_loop(0, n_row // slots, attend, 0)
    others = pl.ds(1, n_row - 1)
    for i in row_far:
        pltpu.make_async_remote_copy(src_ref=lsend.at[i], dst_ref=lrecv.at[i], send_sem=rs.at[1], recv_sem=rr.at[1],
                                     device_id=row_peer(i, -1), device_id_type=MESH).start()
        pltpu.make_async_remote_copy(src_ref=osend.at[i], dst_ref=orecv.at[i], send_sem=rs.at[0], recv_sem=rr.at[0],
                                     device_id=row_peer(i, -1), device_id_type=MESH).start()
    orecv[0] = osend[0]
    lrecv[0] = lsend[0]
    arrived(enc_copies)
    pltpu.make_async_copy(orecv.at[others], orecv.at[others], rr.at[0]).wait()
    pltpu.make_async_copy(lrecv.at[others], lrecv.at[others], rr.at[1]).wait()

    levels = lrecv[...]
    share = jnp.exp(levels - jnp.max(levels, axis=0, keepdims=True))
    share = share / jnp.sum(share, axis=0, keepdims=True)
    spot = iota((n_row, 16, 128), 1) == iota((n_row, 16, 128), 2) % 32
    share = jnp.where(spot, share, 0.0).reshape(n_row * 16, 128)
    high = share.astype(BF)
    low = (share - high.astype(F32)).astype(BF)
    blocks = ((iota((256, 128), 0) % 128) // 32 == iota((256, 128), 1) // 32).astype(F32).astype(BF)
    share = dot(jnp.concatenate([high, low], axis=1), blocks).reshape(n_row, 16, 128)
    attended = jnp.sum(share * orecv[...].astype(F32), axis=0)
    attended = jnp.concatenate([attended[0:8], attended[8:16]], axis=1)
    attended = jnp.concatenate([attended, jnp.zeros_like(attended)], axis=0).astype(BF)
    mixture = tokens_s[...] + dot(attended, ow[...])[0:8]
    mixture = jnp.concatenate([mixture, jnp.zeros_like(mixture)], axis=0).astype(BF)
    r, k = iota((16, 16), 0), iota((16, 16), 1)
    twice = ((r // 8) * 4 + (r % 8) // 2 == k).astype(F32).astype(BF)
    upward = dot(dot(twice, mixture).astype(BF), uw[...])
    odd, right = row8 % 2 == 1, group8 >= 2
    for a in range(2):
        first = upward[0:8, a * 128:a * 128 + 128]
        second = upward[8:16, a * 128:a * 128 + 128]
        plane = jnp.where(right, jnp.where(odd, second, roll(second, 64, 1)), jnp.where(odd, roll(first, 64, 1), first))
        for y in range(8):
            up[a, y, 0] = plane[y:y + 1, :]
            uppad[1 + a, 1 + y, 1] = plane[y:y + 1, :]

    up_copies = []
    for n, (a, b, c) in enumerate(STEPS):
        sx = {-1: pl.ds(0, 1), 0: pl.ds(0, 2), 1: pl.ds(1, 1)}[a]
        dx = {-1: pl.ds(3, 1), 0: pl.ds(1, 2), 1: pl.ds(0, 1)}[a]
        sy = {-1: pl.ds(0, 1), 0: pl.ds(0, 8), 1: pl.ds(7, 1)}[b]
        dy = {-1: pl.ds(9, 1), 0: pl.ds(1, 8), 1: pl.ds(0, 1)}[b]
        up_copies.append(remote(up.at[sx, sy, pl.ds(0, 1)], uppad.at[dx, dy, pl.ds(1 - c, 1)], us.at[n], ur.at[n], (a, b, c)))
    start_all(up_copies)
    arrived(up_copies)

    group1 = iota((1, 128), 1) // 32

    def wide(plane, y):
        middle = uppad[plane, y, 1]
        parts = [uppad[plane, y, 0]]
        for q in range(4):
            part = jnp.where(group1 == q, middle, 0.0)
            part = part + roll(part, 64, 1)
            parts.append(part + roll(part, 32, 1))
        return jnp.concatenate(parts + [uppad[plane, y, 2]], axis=1)

    row_wide = iota((8, 768), 0)
    for plane in range(4):
        xs = (range(0, 1), range(1, 5), range(5, 9), range(9, 10))[plane]
        for y2 in range(2):
            four = [wide(plane, 1 + 4 * y2 + i) for i in range(4)]
            more = jnp.concatenate([jnp.where(row_wide < 4, four[2 * i], four[2 * i + 1]) for i in range(2)], axis=0)
            for x in xs:
                joi[x, 16 * y2:16 * y2 + 16, :] = (enc[x, 16 * y2:16 * y2 + 16, :].astype(F32) + more).astype(BF)
    row_rim = iota((16, 768), 0)
    for rim, full, y in ((enc_lo, joi_lo, 0), (enc_hi, joi_hi, 9)):
        planes = [wide(plane, y) for plane in range(4)]
        full[0] = (rim[0].astype(F32) + planes[0]).astype(BF)
        full[1] = (rim[1].astype(F32) + jnp.where(row_rim < 4, planes[1], planes[2])).astype(BF)
        full[2] = (rim[2].astype(F32) + planes[3]).astype(BF)

    def keep_result(x, h, value):
        out_ref[x, :, 256 * h:256 * h + 256] = value.astype(BF)

    convolve(joi, joi_lo, joi_hi, keep_result)

    departed(vol_copies)
    departed(enc_copies)
    departed(up_copies)
    q_gone.wait()
    kv_gone.wait()
    pltpu.make_async_copy(orecv.at[others], orecv.at[others], rs.at[0]).wait()
    pltpu.make_async_copy(lrecv.at[others], lrecv.at[others], rs.at[1]).wait()


def on_device(sizes, volume, conv_in, conv_out, norm_gain, q_weight, kv_weight, out_weight, up_weight):
    n_row, n_col = (sizes[1] // 2) * sizes[2], sizes[0] * 2
    padded, rim, rows = (10, 32, 768), (3, 16, 768), (2, 16, 512)
    vmem = pltpu.VMEM
    scratch = [vmem((8, 32, 16, 32), BF)] + [vmem(padded, BF), vmem(rim, BF), vmem(rim, BF)] * 3 + [vmem(rows, BF)] * 2
    scratch += [vmem((864, 32), BF)] * 2 + [vmem((1, 256), F32), vmem((256, 256), BF), vmem((256, 512), BF), vmem((256, 256), BF), vmem((256, 256), BF)]
    scratch += [vmem((3, 1536, 256), BF), vmem((544, 1536), BF), vmem((3, 552, 256), F32), vmem((8, 256), F32)]
    scratch += [vmem((n_row, 16, 128), BF), vmem((n_col, 32, 128), BF), vmem((4, n_col * 16, 128), BF), vmem((4, n_col * 16, 256), BF)]
    scratch += [vmem((n_row, 16, 128), BF)] * 2 + [vmem((n_row, 1, 128), F32)] * 2
    scratch += [vmem((2, 8, 1, 1, 128), F32), vmem((4, 10, 3, 1, 128), F32)]
    dma = pltpu.SemaphoreType.DMA
    scratch += [dma((8,))] + [dma((26,))] * 6 + [dma((2,))] * 4
    result = pl.pallas_call(
        functools.partial(kernel, sizes),
        out_shape=jax.ShapeDtypeStruct((8, 32, 512), BF),
        in_specs=[pl.BlockSpec(memory_space=pltpu.HBM)] * 8,
        out_specs=pl.BlockSpec(memory_space=pltpu.VMEM),
        scratch_shapes=scratch,
        compiler_params=pltpu.CompilerParams(collective_id=0, has_side_effects=True, vmem_limit_bytes=48 * 2**20),
    )(*(pltpu.with_memory_space_constraint(a, pltpu.HBM) for a in (volume, conv_in.reshape(864, 32), conv_out.reshape(864, 32), norm_gain.reshape(1, 256), q_weight, kv_weight, out_weight, up_weight)))
    return result.reshape(8, 32, 16, 32)


def solution(mesh):
    placed = (P("gx", "gy", "gz", None), P(), P(), P(), P(), P(), P(), P())
    sizes = tuple(mesh.shape[name] for name in ("gx", "gy", "gz"))
    return jax.shard_map(
        functools.partial(on_device, sizes), mesh=mesh, in_specs=placed, out_specs=P("gx", "gy", "gz", None), check_vma=False
    )
```

```python
import functools

import jax
import jax.numpy as jnp
from jax import lax
from jax.experimental import pallas as pl
from jax.experimental.pallas import tpu as pltpu
from jax.sharding import PartitionSpec as P

BF = jnp.bfloat16
F32 = jnp.float32
MESH = pl.DeviceIdType.MESH
STEPS = [(a, b, c) for a in (-1, 0, 1) for b in (-1, 0, 1) for c in (-1, 0, 1) if (a, b, c) != (0, 0, 0)]
STEPS.sort(key=lambda step: -sum(abs(v) for v in step))


def iota(shape, dim):
    return lax.broadcasted_iota(jnp.int32, shape, dim)


def dot(left, right):
    return jnp.dot(left, right, preferred_element_type=F32)


def roll(value, shift, axis):
    return pltpu.roll(value, shift, axis)


def lane_window(c, width):
    if c == 0:
        return (0, 512), (128, 512)
    if c == 1:
        return (384, 128), (0, 128)
    return (0, 128), (640, 128)


def kernel(sizes, x_hbm, win_hbm, wout_hbm, gain_hbm, qw_hbm, kvw_hbm, ow_hbm, uw_hbm, out_ref,
           raw, vol, vol_lo, vol_hi, enc, enc_lo, enc_hi, joi, joi_lo, joi_hi, rows_v, rows_e,
           win, wout, gain, qw, kvw, ow, uw, taps, lhs, acc, tokens_s,
           qbuf, kvbuf, kmask, vmask, osend, orecv, lsend, lrecv, up, uppad,
           load_sem, vs, vr, es, er, us, ur, gs, gr, rs, rr):
    GX, GY, GZ = sizes
    gx, gy, gz = lax.axis_index("gx"), lax.axis_index("gy"), lax.axis_index("gz")
    n_row, n_col = (GY // 2) * GZ, GX * 2

    def at_mesh(x, y, z):
        return (x, y, z)

    row_y = [(gy + 2 * k) % GY for k in range(GY // 2)]
    row_z = [(gz + k) % GZ for k in range(GZ)]
    col_x = [(gx + k) % GX for k in range(GX)]
    col_y = [gy, gy // 2 * 2 + (gy + 1) % 2]

    def row_peer(i, sign=1):
        return at_mesh(gx, row_y[sign * (i // GZ) % (GY // 2)], row_z[sign * (i % GZ) % GZ])

    def col_peer(i):
        return at_mesh(col_x[i // 2], col_y[i % 2], gz)

    row_far = sorted(range(1, n_row), key=lambda i: -2 * min(i // GZ, GY // 2 - i // GZ) - min(i % GZ // 2, GZ // 2 - i % GZ // 2) - i % 2)
    col_far = sorted(range(1, n_col), key=lambda i: -min(i // 2, GX - i // 2))

    def inside(a, b, c):
        ok = None
        for at, step, size in ((gx, a, GX), (gy, b, GY), (gz, c, GZ)):
            if step:
                here = at < size - 1 if step > 0 else at > 0
                ok = here if ok is None else ok & here
        return ok

    def neighbour(a, b, c):
        return at_mesh(gx + a, gy + b, gz + c)

    for ref in (vol, enc):
        for x in (0, 9):
            ref[x] = jnp.zeros((32, 768), BF)
        for z in (0, 640):
            ref[1:9, :, z:z + 128] = jnp.zeros((8, 32, 128), BF)
    for ref in (vol_lo, vol_hi, enc_lo, enc_hi, uppad):
        ref[...] = jnp.zeros(ref.shape, ref.dtype)
    barrier = pltpu.get_barrier_semaphore()
    for step in STEPS:
        @pl.when(inside(*step))
        def _(step=step):
            pl.semaphore_signal(barrier, inc=1, device_id=neighbour(*step), device_id_type=MESH)
    for i in range(1, n_row):
        pl.semaphore_signal(barrier, inc=1, device_id=row_peer(i), device_id_type=MESH)
    for i in range(1, n_col):
        pl.semaphore_signal(barrier, inc=1, device_id=col_peer(i), device_id_type=MESH)

    own = (pl.ds(1, 8), pl.ds(0, 32), pl.ds(128, 512))
    loads = [pltpu.make_async_copy(x_hbm, raw, load_sem.at[0])]
    pairs = [(win_hbm, win), (wout_hbm, wout), (gain_hbm, gain), (qw_hbm, qw), (kvw_hbm, kvw), (ow_hbm, ow), (uw_hbm, uw)]
    loads += [pltpu.make_async_copy(s, d, load_sem.at[i + 1]) for i, (s, d) in enumerate(pairs)]
    for copy in loads:
        copy.start()

    def pack_rows(main, rows):
        r, k = iota((32, 256), 0), iota((32, 256), 1)
        wanted = jnp.where(r < 16, r * 32, (r - 16) * 32 + 31)
        picked = dot((wanted == k).astype(F32).astype(BF), main[own].reshape(256, 512))
        rows[...] = picked.astype(BF).reshape(2, 16, 512)

    def remote(src, dst, send, recv, step):
        copy = pltpu.make_async_remote_copy(src_ref=src, dst_ref=dst, send_sem=send, recv_sem=recv,
                                            device_id=neighbour(*step), device_id_type=MESH)
        return copy, pltpu.make_async_copy(dst, dst, recv), pltpu.make_async_copy(src, src, send)

    def halo_copies(main, rows, lo, hi, send, recv):
        copies = []
        for n, (a, b, c) in enumerate(STEPS):
            (s0, width), (d0, _) = lane_window(c, 512)
            if b == 0:
                sx = {-1: pl.ds(1, 1), 0: pl.ds(1, 8), 1: pl.ds(8, 1)}[a]
                dx = {-1: pl.ds(9, 1), 0: pl.ds(1, 8), 1: pl.ds(0, 1)}[a]
                src = main.at[sx, pl.ds(0, 32), pl.ds(128 + s0, width)]
                dst = main.at[dx, pl.ds(0, 32), pl.ds(d0, width)]
            else:
                src = rows.at[1 if b == 1 else 0, pl.ds(0, 16), pl.ds(s0, width)]
                dst = (lo if b == 1 else hi).at[1 - a, pl.ds(0, 16), pl.ds(d0, width)]
            copies.append(remote(src, dst, send.at[n], recv.at[n], (a, b, c)))
        return copies

    def start_all(copies):
        for step, (copy, _, _) in zip(STEPS, copies):
            @pl.when(inside(*step))
            def _(copy=copy):
                copy.start()

    def arrived(copies):
        for (a, b, c), (_, landing, _) in zip(STEPS, copies):
            @pl.when(inside(-a, -b, -c))
            def _(landing=landing):
                landing.wait()

    def departed(copies):
        for step, (_, _, leaving) in zip(STEPS, copies):
            @pl.when(inside(*step))
            def _(leaving=leaving):
                leaving.wait()

    def spread_taps(w):
        k, n = iota((32, 512), 0), iota((32, 512), 1)
        place = ((n % 32 == k) & (n // 128 == (n % 128) // 32)).astype(F32).astype(BF)
        moved = dot(w[...], place).astype(BF)
        taps[...] = jnp.zeros(taps.shape, BF)
        for dx in range(3):
            for dy in range(3):
                first = (dx * 3 + dy) * 96
                for m in range(2):
                    for z in range(8):
                        total = None
                        for g in range(4):
                            dz = z - 4 * m - g + 1
                            if 0 <= dz <= 2:
                                piece = moved[first + dz * 32:first + dz * 32 + 32, g * 128:g * 128 + 128]
                                total = piece if total is None else total + piece
                        if total is not None:
                            r0 = dx * 256 + z * 32
                            taps[dy, r0:r0 + 32, m * 128:m * 128 + 128] = total
                above, below = 768 + 32 * (0, 2, 4)[dx], 768 + 32 * (3, 1, 7)[dx]
                taps[dy, above:above + 32, 128:256] = moved[first + 64:first + 96, 384:512]
                taps[dy, below:below + 32, 0:128] = moved[first:first + 32, 0:128]

    def convolve(main, lo, hi, emit):
        row8 = iota((8, 768), 0)

        def three(rim):
            before, here, after = (rim[i].astype(F32)[0:8] for i in range(3))
            return (jnp.where(row8 == 0, roll(before, 1, 0), roll(here, 1, 0)), here,
                    jnp.where(row8 == 7, roll(after, 7, 0), roll(here, 7, 0)))

        rims = [jnp.concatenate(p, axis=0) for p in zip(three(lo), three(hi))]
        g = iota((1, 128), 1) // 32
        last, first = (g == 3).astype(F32), (g == 0).astype(F32)
        for h, (a, b) in enumerate(((0, 384), (256, 640))):
            rows, few = slice(h * 256, h * 256 + 256), slice(512 + 16 * h, 528 + 16 * h)
            o = 128 + 256 * h
            for dx in range(3):
                lhs[rows, dx * 256:dx * 256 + 256] = main[dx:dx + 8, :, o:o + 256].reshape(256, 256)
                lhs[few, dx * 256:dx * 256 + 256] = rims[dx][:, o:o + 256].astype(BF)
            ends = (main[:, :, a:a + 128].reshape(320, 128) * last.astype(BF) + main[:, :, b:b + 128].reshape(320, 128) * first.astype(BF))
            turned = roll(ends[32:288].astype(F32), 64, 1).astype(BF)
            lhs[rows, 768:896] = ends[0:256] + turned
            lhs[rows, 896:1024] = ends[64:320]
            ends = [rim[:, a:a + 128] * last + rim[:, b:b + 128] * first for rim in rims]
            lhs[few, 768:896] = (ends[0] + roll(ends[1], 64, 1)).astype(BF)
            lhs[few, 896:1024] = ends[2].astype(BF)

        def one(dy, carry):
            acc[dy, 0:544, :] = dot(lhs[...], taps[dy])
            return carry

        lax.fori_loop(0, 3, one, 0)
        row = iota((32, 256), 0)

        def join(x, carry):
            for h in range(2):
                at = pl.ds(pl.multiple_of(h * 256 + x * 32, 32), 32)
                below = jnp.where(row == 0, acc[0, pl.ds(512 + 16 * h + x, 1), :], roll(acc[0, at, :], 1, 0))
                above = jnp.where(row == 31, acc[2, pl.ds(520 + 16 * h + x, 1), :], roll(acc[2, at, :], 31, 0))
                emit(x, h, below + acc[1, at, :] + above)
            return carry

        lax.fori_loop(0, 8, join, 0)

    loads[0].wait()
    for x in range(8):
        vol[1 + x, :, 128:640] = raw[x].reshape(32, 512)
    pack_rows(vol, rows_v)
    neighbours = (1 + (gx > 0).astype(jnp.int32) + (gx < GX - 1).astype(jnp.int32))
    neighbours *= (1 + (gy > 0).astype(jnp.int32) + (gy < GY - 1).astype(jnp.int32))
    neighbours *= (1 + (gz > 0).astype(jnp.int32) + (gz < GZ - 1).astype(jnp.int32))
    pl.semaphore_wait(barrier, neighbours - 1 + n_row - 1 + n_col - 1)
    vol_copies = halo_copies(vol, rows_v, vol_lo, vol_hi, vs, vr)
    start_all(vol_copies)
    for copy in loads[1:]:
        copy.wait()
    spread_taps(win)
    arrived(vol_copies)

    def keep_encoded(x, h, value):
        enc[1 + x, :, 128 + 256 * h:384 + 256 * h] = jnp.maximum(value, 0.0).astype(BF)

    convolve(vol, vol_lo, vol_hi, keep_encoded)

    r, k = iota((32, 256), 0), iota((32, 256), 1)
    pool = ((k // 128 == r // 16) & ((k % 32) // 4 == 2 * (r % 4) + (r // 8) % 2)).astype(F32).astype(BF)
    sums = dot(pool, enc[own].reshape(256, 512))
    row8, group8 = iota((8, 128), 0), iota((8, 128), 1) // 32
    chunks = []
    for q in range(4):
        part = sums[:, q * 128:q * 128 + 128]
        part = part + roll(part, 64, 1)
        chunks.append(part + roll(part, 32, 1))

    def cell(ab, c):
        return jnp.where(row8 < 4, chunks[c][ab * 8:ab * 8 + 8], chunks[2 + c][ab * 8:ab * 8 + 8])

    sides = []
    for a in range(2):
        side = cell(2 * a + 1, 1)
        for n, (b, c) in enumerate(((0, 0), (0, 1), (1, 0))):
            side = jnp.where(group8 == n, cell(2 * a + b, c), side)
        sides.append(side)
    tokens = jnp.concatenate(sides, axis=1) * (1.0 / 64.0)
    tokens_s[...] = tokens
    center = tokens - jnp.mean(tokens, axis=1, keepdims=True)
    variance = jnp.mean(center * center, axis=1, keepdims=True)
    normed = center * lax.rsqrt(variance + 1e-05) * gain[...]
    normed = jnp.concatenate([normed, jnp.zeros_like(normed)], axis=0).astype(BF)
    queries = dot(normed, qw[...])[0:8]
    key_value = dot(normed, kvw[...])[0:8]
    qbuf[0] = jnp.concatenate([queries[:, i * 128:i * 128 + 128] for i in range(2)], axis=0).astype(BF)
    kvbuf[0] = jnp.concatenate([key_value[:, i * 128:i * 128 + 128] for i in range(4)], axis=0).astype(BF)

    q_all = pltpu.make_async_copy(qbuf.at[pl.ds(1, n_row - 1)], qbuf.at[pl.ds(1, n_row - 1)], gr.at[0])
    kv_all = pltpu.make_async_copy(kvbuf.at[pl.ds(1, n_col - 1)], kvbuf.at[pl.ds(1, n_col - 1)], gr.at[1])
    q_gone = pltpu.make_async_copy(qbuf.at[pl.ds(1, n_row - 1)], qbuf.at[pl.ds(1, n_row - 1)], gs.at[0])
    kv_gone = pltpu.make_async_copy(kvbuf.at[pl.ds(1, n_col - 1)], kvbuf.at[pl.ds(1, n_col - 1)], gs.at[1])
    sends = [(n / len(row_far), qbuf, 0, i, row_peer(i)) for n, i in enumerate(row_far)]
    sends += [(n / len(col_far), kvbuf, 1, i, col_peer(i)) for n, i in enumerate(col_far)]
    for _, buf, n, i, peer in sorted(sends, key=lambda s: s[0]):
        pltpu.make_async_remote_copy(src_ref=buf.at[0], dst_ref=buf.at[i], send_sem=gs.at[n], recv_sem=gr.at[n],
                                     device_id=peer, device_id_type=MESH).start()
    pack_rows(enc, rows_e)
    enc_copies = halo_copies(enc, rows_e, enc_lo, enc_hi, es, er)
    start_all(enc_copies)
    spread_taps(wout)

    q_all.wait()
    kv_all.wait()
    n_keys = n_col * 16
    lane_group = iota((n_keys, 128), 1) // 32
    keys = kvbuf[:, 0:16, :].reshape(n_keys, 128)
    values = kvbuf[:, 16:32, :].reshape(n_keys, 128)
    for g in range(4):
        mine = (lane_group == g).astype(F32).astype(BF)
        kmask[g] = keys * mine
        vmask[g, :, 0:128] = values * mine
        vmask[g, :, 128:256] = mine
    slots = min(8, n_row)
    n_rows = slots * 16
    same_half = (iota((n_rows, n_keys), 0) // 8) % 2 == (iota((n_rows, n_keys), 1) // 8) % 2
    group = iota((n_rows, 128), 1) // 32
    compact = iota((slots, 16, 128), 1) == iota((slots, 16, 128), 2) % 32

    def attend(i, carry):
        at = pl.ds(i * slots, slots)
        query = qbuf[at].reshape(n_rows, 128)
        total, peaks = jnp.zeros((n_rows, 256), F32), jnp.zeros((n_rows, 128), F32)
        for g in range(4):
            scores = lax.dot_general(query, kmask[g], (((1,), (1,)), ((), ())), preferred_element_type=F32)
            scores = jnp.where(same_half, scores * 32 ** (-0.5), -1e30)
            peak = jnp.max(scores, axis=1, keepdims=True)
            total = total + dot(jnp.exp(scores - peak).astype(BF), vmask[g])
            peaks = jnp.where(group == g, peak, peaks)
        weight = total[:, 128:256]
        osend[at] = (total[:, 0:128] / weight).astype(BF).reshape(slots, 16, 128)
        level = (peaks + jnp.log(weight)).reshape(slots, 16, 128)
        lsend[at] = jnp.sum(jnp.where(compact, level, 0.0), axis=1, keepdims=True)
        return carry

    lax.fori_loop(0, n_row // slots, attend, 0)
    others = pl.ds(1, n_row - 1)
    for i in row_far:
        pltpu.make_async_remote_copy(src_ref=lsend.at[i], dst_ref=lrecv.at[i], send_sem=rs.at[1], recv_sem=rr.at[1],
                                     device_id=row_peer(i, -1), device_id_type=MESH).start()
        pltpu.make_async_remote_copy(src_ref=osend.at[i], dst_ref=orecv.at[i], send_sem=rs.at[0], recv_sem=rr.at[0],
                                     device_id=row_peer(i, -1), device_id_type=MESH).start()
    orecv[0] = osend[0]
    lrecv[0] = lsend[0]
    arrived(enc_copies)
    pltpu.make_async_copy(orecv.at[others], orecv.at[others], rr.at[0]).wait()
    pltpu.make_async_copy(lrecv.at[others], lrecv.at[others], rr.at[1]).wait()

    levels = lrecv[...]
    share = jnp.exp(levels - jnp.max(levels, axis=0, keepdims=True))
    share = share / jnp.sum(share, axis=0, keepdims=True)
    spot = iota((n_row, 16, 128), 1) == iota((n_row, 16, 128), 2) % 32
    share = jnp.where(spot, share, 0.0).reshape(n_row * 16, 128)
    high = share.astype(BF)
    low = (share - high.astype(F32)).astype(BF)
    blocks = ((iota((256, 128), 0) % 128) // 32 == iota((256, 128), 1) // 32).astype(F32).astype(BF)
    share = dot(jnp.concatenate([high, low], axis=1), blocks).reshape(n_row, 16, 128)
    attended = jnp.sum(share * orecv[...].astype(F32), axis=0)
    attended = jnp.concatenate([attended[0:8], attended[8:16]], axis=1)
    attended = jnp.concatenate([attended, jnp.zeros_like(attended)], axis=0).astype(BF)
    mixture = tokens_s[...] + dot(attended, ow[...])[0:8]
    mixture = jnp.concatenate([mixture, jnp.zeros_like(mixture)], axis=0).astype(BF)
    r, k = iota((16, 16), 0), iota((16, 16), 1)
    twice = ((r // 8) * 4 + (r % 8) // 2 == k).astype(F32).astype(BF)
    upward = dot(dot(twice, mixture).astype(BF), uw[...])
    odd, right = row8 % 2 == 1, group8 >= 2
    for a in range(2):
        first = upward[0:8, a * 128:a * 128 + 128]
        second = upward[8:16, a * 128:a * 128 + 128]
        plane = jnp.where(right, jnp.where(odd, second, roll(second, 64, 1)), jnp.where(odd, roll(first, 64, 1), first))
        for y in range(8):
            up[a, y, 0] = plane[y:y + 1, :]
            uppad[1 + a, 1 + y, 1] = plane[y:y + 1, :]

    up_copies = []
    for n, (a, b, c) in enumerate(STEPS):
        sx = {-1: pl.ds(0, 1), 0: pl.ds(0, 2), 1: pl.ds(1, 1)}[a]
        dx = {-1: pl.ds(3, 1), 0: pl.ds(1, 2), 1: pl.ds(0, 1)}[a]
        sy = {-1: pl.ds(0, 1), 0: pl.ds(0, 8), 1: pl.ds(7, 1)}[b]
        dy = {-1: pl.ds(9, 1), 0: pl.ds(1, 8), 1: pl.ds(0, 1)}[b]
        up_copies.append(remote(up.at[sx, sy, pl.ds(0, 1)], uppad.at[dx, dy, pl.ds(1 - c, 1)], us.at[n], ur.at[n], (a, b, c)))
    start_all(up_copies)
    departed(vol_copies)
    departed(enc_copies)
    departed(up_copies)
    q_gone.wait()
    kv_gone.wait()
    pltpu.make_async_copy(orecv.at[others], orecv.at[others], rs.at[0]).wait()
    pltpu.make_async_copy(lrecv.at[others], lrecv.at[others], rs.at[1]).wait()
    arrived(up_copies)

    group1 = iota((1, 128), 1) // 32

    def wide(plane, y):
        middle = uppad[plane, y, 1]
        parts = [uppad[plane, y, 0]]
        for q in range(4):
            part = jnp.where(group1 == q, middle, 0.0)
            part = part + roll(part, 64, 1)
            parts.append(part + roll(part, 32, 1))
        return jnp.concatenate(parts + [uppad[plane, y, 2]], axis=1)

    row_wide = iota((8, 768), 0)
    for plane in range(4):
        xs = (range(0, 1), range(1, 5), range(5, 9), range(9, 10))[plane]
        for y2 in range(2):
            four = [wide(plane, 1 + 4 * y2 + i) for i in range(4)]
            more = jnp.concatenate([jnp.where(row_wide < 4, four[2 * i], four[2 * i + 1]) for i in range(2)], axis=0)
            for x in xs:
                joi[x, 16 * y2:16 * y2 + 16, :] = (enc[x, 16 * y2:16 * y2 + 16, :].astype(F32) + more).astype(BF)
    row_rim = iota((16, 768), 0)
    for rim, full, y in ((enc_lo, joi_lo, 0), (enc_hi, joi_hi, 9)):
        planes = [wide(plane, y) for plane in range(4)]
        full[0] = (rim[0].astype(F32) + planes[0]).astype(BF)
        full[1] = (rim[1].astype(F32) + jnp.where(row_rim < 4, planes[1], planes[2])).astype(BF)
        full[2] = (rim[2].astype(F32) + planes[3]).astype(BF)

    def keep_result(x, h, value):
        out_ref[x, :, 256 * h:256 * h + 256] = value.astype(BF)

    convolve(joi, joi_lo, joi_hi, keep_result)


def on_device(sizes, volume, conv_in, conv_out, norm_gain, q_weight, kv_weight, out_weight, up_weight):
    n_row, n_col = (sizes[1] // 2) * sizes[2], sizes[0] * 2
    padded, rim, rows = (10, 32, 768), (3, 16, 768), (2, 16, 512)
    vmem = pltpu.VMEM
    scratch = [vmem((8, 32, 16, 32), BF)] + [vmem(padded, BF), vmem(rim, BF), vmem(rim, BF)] * 3 + [vmem(rows, BF)] * 2
    scratch += [vmem((864, 32), BF)] * 2 + [vmem((1, 256), F32), vmem((256, 256), BF), vmem((256, 512), BF), vmem((256, 256), BF), vmem((256, 256), BF)]
    scratch += [vmem((3, 1024, 256), BF), vmem((544, 1024), BF), vmem((3, 552, 256), F32), vmem((8, 256), F32)]
    scratch += [vmem((n_row, 16, 128), BF), vmem((n_col, 32, 128), BF), vmem((4, n_col * 16, 128), BF), vmem((4, n_col * 16, 256), BF)]
    scratch += [vmem((n_row, 16, 128), BF)] * 2 + [vmem((n_row, 1, 128), F32)] * 2
    scratch += [vmem((2, 8, 1, 1, 128), F32), vmem((4, 10, 3, 1, 128), F32)]
    dma = pltpu.SemaphoreType.DMA
    scratch += [dma((8,))] + [dma((26,))] * 6 + [dma((2,))] * 4
    result = pl.pallas_call(
        functools.partial(kernel, sizes),
        out_shape=jax.ShapeDtypeStruct((8, 32, 512), BF),
        in_specs=[pl.BlockSpec(memory_space=pltpu.HBM)] * 8,
        out_specs=pl.BlockSpec(memory_space=pltpu.VMEM),
        scratch_shapes=scratch,
        compiler_params=pltpu.CompilerParams(collective_id=0, has_side_effects=True, vmem_limit_bytes=48 * 2**20),
    )(*(pltpu.with_memory_space_constraint(a, pltpu.HBM) for a in (volume, conv_in.reshape(864, 32), conv_out.reshape(864, 32), norm_gain.reshape(1, 256), q_weight, kv_weight, out_weight, up_weight)))
    return result.reshape(8, 32, 16, 32)


def solution(mesh):
    placed = (P("gx", "gy", "gz", None), P(), P(), P(), P(), P(), P(), P())
    sizes = tuple(mesh.shape[name] for name in ("gx", "gy", "gz"))
    return jax.shard_map(
        functools.partial(on_device, sizes), mesh=mesh, in_specs=placed, out_specs=P("gx", "gy", "gz", None), check_vma=False
    )
```

```python
import functools

import jax
import jax.numpy as jnp
from jax import lax
from jax.experimental import pallas as pl
from jax.experimental.pallas import tpu as pltpu
from jax.sharding import PartitionSpec as P

BF = jnp.bfloat16
F32 = jnp.float32
MESH = pl.DeviceIdType.MESH
STEPS = [(a, b, c) for a in (-1, 0, 1) for b in (-1, 0, 1) for c in (-1, 0, 1) if (a, b, c) != (0, 0, 0)]
STEPS.sort(key=lambda step: -sum(abs(v) for v in step))


def iota(shape, dim):
    return lax.broadcasted_iota(jnp.int32, shape, dim)


def dot(left, right):
    return jnp.dot(left, right, preferred_element_type=F32)


def roll(value, shift, axis):
    return pltpu.roll(value, shift, axis)


def lane_window(c, width):
    if c == 0:
        return (0, 512), (128, 512)
    if c == 1:
        return (384, 128), (0, 128)
    return (0, 128), (640, 128)


def kernel(sizes, x_hbm, win_hbm, wout_hbm, gain_hbm, qw_hbm, kvw_hbm, ow_hbm, uw_hbm, out_ref,
           raw, vol, vol_lo, vol_hi, enc, enc_lo, enc_hi, joi, joi_lo, joi_hi, rows_v, rows_e,
           win, wout, gain, qw, kvw, ow, uw, taps, lhs, acc, tokens_s,
           qbuf, kvbuf, kmask, vmask, osend, orecv, lsend, lrecv, up, uppad,
           load_sem, vs, vr, es, er, us, ur, gs, gr, rs, rr):
    GX, GY, GZ = sizes
    gx, gy, gz = lax.axis_index("gx"), lax.axis_index("gy"), lax.axis_index("gz")
    n_row, n_col = (GY // 2) * GZ, GX * 2

    def at_mesh(x, y, z):
        return (x, y, z)

    row_y = [(gy + 2 * k) % GY for k in range(GY // 2)]
    row_z = [(gz + k) % GZ for k in range(GZ)]
    col_x = [(gx + k) % GX for k in range(GX)]
    col_y = [gy, gy // 2 * 2 + (gy + 1) % 2]

    def row_peer(i, sign=1):
        return at_mesh(gx, row_y[sign * (i // GZ) % (GY // 2)], row_z[sign * (i % GZ) % GZ])

    def col_peer(i):
        return at_mesh(col_x[i // 2], col_y[i % 2], gz)

    row_far = sorted(range(1, n_row), key=lambda i: -2 * min(i // GZ, GY // 2 - i // GZ) - min(i % GZ // 2, GZ // 2 - i % GZ // 2) - i % 2)
    col_far = sorted(range(1, n_col), key=lambda i: -min(i // 2, GX - i // 2))

    def inside(a, b, c):
        ok = None
        for at, step, size in ((gx, a, GX), (gy, b, GY), (gz, c, GZ)):
            if step:
                here = at < size - 1 if step > 0 else at > 0
                ok = here if ok is None else ok & here
        return ok

    def neighbour(a, b, c):
        return at_mesh(gx + a, gy + b, gz + c)

    for ref in (vol, enc):
        for x in (0, 9):
            ref[x] = jnp.zeros((32, 768), BF)
        for z in (0, 640):
            ref[1:9, :, z:z + 128] = jnp.zeros((8, 32, 128), BF)
    for ref in (vol_lo, vol_hi, enc_lo, enc_hi, uppad):
        ref[...] = jnp.zeros(ref.shape, ref.dtype)
    barrier = pltpu.get_barrier_semaphore()
    for i in row_far:
        pl.semaphore_signal(barrier, inc=1, device_id=row_peer(i), device_id_type=MESH)
    for i in col_far:
        pl.semaphore_signal(barrier, inc=1, device_id=col_peer(i), device_id_type=MESH)
    for step in STEPS:
        @pl.when(inside(*step))
        def _(step=step):
            pl.semaphore_signal(barrier, inc=1, device_id=neighbour(*step), device_id_type=MESH)

    own = (pl.ds(1, 8), pl.ds(0, 32), pl.ds(128, 512))
    loads = [pltpu.make_async_copy(x_hbm, raw, load_sem.at[0])]
    pairs = [(win_hbm, win), (wout_hbm, wout), (gain_hbm, gain), (qw_hbm, qw), (kvw_hbm, kvw), (ow_hbm, ow), (uw_hbm, uw)]
    loads += [pltpu.make_async_copy(s, d, load_sem.at[i + 1]) for i, (s, d) in enumerate(pairs)]
    for copy in loads:
        copy.start()

    def pack_rows(main, rows):
        r, k = iota((32, 256), 0), iota((32, 256), 1)
        wanted = jnp.where(r < 16, r * 32, (r - 16) * 32 + 31)
        picked = dot((wanted == k).astype(F32).astype(BF), main[own].reshape(256, 512))
        rows[...] = picked.astype(BF).reshape(2, 16, 512)

    def remote(src, dst, send, recv, step):
        copy = pltpu.make_async_remote_copy(src_ref=src, dst_ref=dst, send_sem=send, recv_sem=recv,
                                            device_id=neighbour(*step), device_id_type=MESH)
        return copy, pltpu.make_async_copy(dst, dst, recv), pltpu.make_async_copy(src, src, send)

    def halo_copies(main, rows, lo, hi, send, recv):
        copies = []
        for n, (a, b, c) in enumerate(STEPS):
            (s0, width), (d0, _) = lane_window(c, 512)
            if b == 0:
                sx = {-1: pl.ds(1, 1), 0: pl.ds(1, 8), 1: pl.ds(8, 1)}[a]
                dx = {-1: pl.ds(9, 1), 0: pl.ds(1, 8), 1: pl.ds(0, 1)}[a]
                src = main.at[sx, pl.ds(0, 32), pl.ds(128 + s0, width)]
                dst = main.at[dx, pl.ds(0, 32), pl.ds(d0, width)]
            else:
                src = rows.at[1 if b == 1 else 0, pl.ds(0, 16), pl.ds(s0, width)]
                dst = (lo if b == 1 else hi).at[1 - a, pl.ds(0, 16), pl.ds(d0, width)]
            copies.append(remote(src, dst, send.at[n], recv.at[n], (a, b, c)))
        return copies

    def start_all(copies):
        for step, (copy, _, _) in zip(STEPS, copies):
            @pl.when(inside(*step))
            def _(copy=copy):
                copy.start()

    def arrived(copies):
        for (a, b, c), (_, landing, _) in zip(STEPS, copies):
            @pl.when(inside(-a, -b, -c))
            def _(landing=landing):
                landing.wait()

    def departed(copies):
        for step, (_, _, leaving) in zip(STEPS, copies):
            @pl.when(inside(*step))
            def _(leaving=leaving):
                leaving.wait()

    def spread_taps(w):
        k, n = iota((32, 512), 0), iota((32, 512), 1)
        place = ((n % 32 == k) & (n // 128 == (n % 128) // 32)).astype(F32).astype(BF)
        moved = dot(w[...], place).astype(BF)
        taps[...] = jnp.zeros(taps.shape, BF)
        for dx in range(3):
            for dy in range(3):
                first = (dx * 3 + dy) * 96
                for m in range(2):
                    for z in range(8):
                        total = None
                        for g in range(4):
                            dz = z - 4 * m - g + 1
                            if 0 <= dz <= 2:
                                piece = moved[first + dz * 32:first + dz * 32 + 32, g * 128:g * 128 + 128]
                                total = piece if total is None else total + piece
                        if total is not None:
                            r0 = dx * 256 + z * 32
                            taps[dy, r0:r0 + 32, m * 128:m * 128 + 128] = total
                above, below = 768 + 32 * (0, 2, 4)[dx], 768 + 32 * (3, 1, 7)[dx]
                taps[dy, above:above + 32, 128:256] = moved[first + 64:first + 96, 384:512]
                taps[dy, below:below + 32, 0:128] = moved[first:first + 32, 0:128]

    def lay_own(main):
        for h in range(2):
            o = 128 + 256 * h
            for dx, x0, x1 in ((0, 1, 8), (1, 0, 8), (2, 0, 7)):
                planes = main[x0 + dx:x1 + dx, :, o:o + 256].reshape((x1 - x0) * 32, 256)
                lhs[h * 256 + 32 * x0:h * 256 + 32 * x1, dx * 256:dx * 256 + 256] = planes

    def convolve(main, lo, hi, emit):
        row8 = iota((8, 768), 0)

        def three(rim):
            before, here, after = (rim[i].astype(F32)[0:8] for i in range(3))
            return (jnp.where(row8 == 0, roll(before, 1, 0), roll(here, 1, 0)), here,
                    jnp.where(row8 == 7, roll(after, 7, 0), roll(here, 7, 0)))

        rims = [jnp.concatenate(p, axis=0) for p in zip(three(lo), three(hi))]
        g = iota((1, 128), 1) // 32
        last, first = (g == 3).astype(F32), (g == 0).astype(F32)
        for h, (a, b) in enumerate(((0, 384), (256, 640))):
            rows, few = slice(h * 256, h * 256 + 256), slice(512 + 16 * h, 528 + 16 * h)
            o = 128 + 256 * h
            for dx in range(3):
                if dx != 1:
                    edge, plane = (h * 256, 0) if dx == 0 else (h * 256 + 224, 9)
                    lhs[edge:edge + 32, dx * 256:dx * 256 + 256] = main[plane, :, o:o + 256]
                lhs[few, dx * 256:dx * 256 + 256] = rims[dx][:, o:o + 256].astype(BF)
            ends = (main[:, :, a:a + 128].reshape(320, 128) * last.astype(BF) + main[:, :, b:b + 128].reshape(320, 128) * first.astype(BF))
            turned = roll(ends[32:288].astype(F32), 64, 1).astype(BF)
            lhs[rows, 768:896] = ends[0:256] + turned
            lhs[rows, 896:1024] = ends[64:320]
            ends = [rim[:, a:a + 128] * last + rim[:, b:b + 128] * first for rim in rims]
            lhs[few, 768:896] = (ends[0] + roll(ends[1], 64, 1)).astype(BF)
            lhs[few, 896:1024] = ends[2].astype(BF)

        def one(dy, carry):
            acc[dy, 0:544, :] = dot(lhs[...], taps[dy])
            return carry

        lax.fori_loop(0, 3, one, 0)
        row = iota((32, 256), 0)

        def join(x, carry):
            for h in range(2):
                at = pl.ds(pl.multiple_of(h * 256 + x * 32, 32), 32)
                below = jnp.where(row == 0, acc[0, pl.ds(512 + 16 * h + x, 1), :], roll(acc[0, at, :], 1, 0))
                above = jnp.where(row == 31, acc[2, pl.ds(520 + 16 * h + x, 1), :], roll(acc[2, at, :], 31, 0))
                emit(x, h, below + acc[1, at, :] + above)
            return carry

        lax.fori_loop(0, 8, join, 0)

    loads[0].wait()
    for x in range(8):
        vol[1 + x, :, 128:640] = raw[x].reshape(32, 512)
    pack_rows(vol, rows_v)
    neighbours = (1 + (gx > 0).astype(jnp.int32) + (gx < GX - 1).astype(jnp.int32))
    neighbours *= (1 + (gy > 0).astype(jnp.int32) + (gy < GY - 1).astype(jnp.int32))
    neighbours *= (1 + (gz > 0).astype(jnp.int32) + (gz < GZ - 1).astype(jnp.int32))
    pl.semaphore_wait(barrier, neighbours - 1 + n_row - 1 + n_col - 1)
    vol_copies = halo_copies(vol, rows_v, vol_lo, vol_hi, vs, vr)
    start_all(vol_copies)
    for copy in loads[1:]:
        copy.wait()
    lay_own(vol)
    spread_taps(win)
    arrived(vol_copies)

    def keep_encoded(x, h, value):
        enc[1 + x, :, 128 + 256 * h:384 + 256 * h] = jnp.maximum(value, 0.0).astype(BF)

    convolve(vol, vol_lo, vol_hi, keep_encoded)

    r, k = iota((32, 256), 0), iota((32, 256), 1)
    pool = ((k // 128 == r // 16) & ((k % 32) // 4 == 2 * (r % 4) + (r // 8) % 2)).astype(F32).astype(BF)
    sums = dot(pool, enc[own].reshape(256, 512))
    row8, group8 = iota((8, 128), 0), iota((8, 128), 1) // 32
    chunks = []
    for q in range(4):
        part = sums[:, q * 128:q * 128 + 128]
        part = part + roll(part, 64, 1)
        chunks.append(part + roll(part, 32, 1))

    def cell(ab, c):
        return jnp.where(row8 < 4, chunks[c][ab * 8:ab * 8 + 8], chunks[2 + c][ab * 8:ab * 8 + 8])

    sides = []
    for a in range(2):
        side = cell(2 * a + 1, 1)
        for n, (b, c) in enumerate(((0, 0), (0, 1), (1, 0))):
            side = jnp.where(group8 == n, cell(2 * a + b, c), side)
        sides.append(side)
    tokens = jnp.concatenate(sides, axis=1) * (1.0 / 64.0)
    tokens_s[...] = tokens
    center = tokens - jnp.mean(tokens, axis=1, keepdims=True)
    variance = jnp.mean(center * center, axis=1, keepdims=True)
    normed = center * lax.rsqrt(variance + 1e-05) * gain[...]
    normed = jnp.concatenate([normed, jnp.zeros_like(normed)], axis=0).astype(BF)
    queries = dot(normed, qw[...])[0:8]
    key_value = dot(normed, kvw[...])[0:8]
    qbuf[0] = jnp.concatenate([queries[:, i * 128:i * 128 + 128] for i in range(2)], axis=0).astype(BF)
    kvbuf[0] = jnp.concatenate([key_value[:, i * 128:i * 128 + 128] for i in range(4)], axis=0).astype(BF)

    q_all = pltpu.make_async_copy(qbuf.at[pl.ds(1, n_row - 1)], qbuf.at[pl.ds(1, n_row - 1)], gr.at[0])
    kv_all = pltpu.make_async_copy(kvbuf.at[pl.ds(1, n_col - 1)], kvbuf.at[pl.ds(1, n_col - 1)], gr.at[1])
    q_gone = pltpu.make_async_copy(qbuf.at[pl.ds(1, n_row - 1)], qbuf.at[pl.ds(1, n_row - 1)], gs.at[0])
    kv_gone = pltpu.make_async_copy(kvbuf.at[pl.ds(1, n_col - 1)], kvbuf.at[pl.ds(1, n_col - 1)], gs.at[1])
    sends = [(n / len(row_far), qbuf, 0, i, row_peer(i)) for n, i in enumerate(row_far)]
    sends += [(n / len(col_far), kvbuf, 1, i, col_peer(i)) for n, i in enumerate(col_far)]
    for _, buf, n, i, peer in sorted(sends, key=lambda s: s[0]):
        pltpu.make_async_remote_copy(src_ref=buf.at[0], dst_ref=buf.at[i], send_sem=gs.at[n], recv_sem=gr.at[n],
                                     device_id=peer, device_id_type=MESH).start()
    pack_rows(enc, rows_e)
    enc_copies = halo_copies(enc, rows_e, enc_lo, enc_hi, es, er)
    start_all(enc_copies)
    spread_taps(wout)

    q_all.wait()
    kv_all.wait()
    n_keys = n_col * 16
    lane_group = iota((n_keys, 128), 1) // 32
    keys = kvbuf[:, 0:16, :].reshape(n_keys, 128)
    values = kvbuf[:, 16:32, :].reshape(n_keys, 128)
    for g in range(4):
        mine = (lane_group == g).astype(F32).astype(BF)
        kmask[g] = keys * mine
        vmask[g, :, 0:128] = values * mine
        vmask[g, :, 128:256] = mine
    slots = min(8, n_row)
    n_rows = slots * 16
    same_half = (iota((n_rows, n_keys), 0) // 8) % 2 == (iota((n_rows, n_keys), 1) // 8) % 2
    group = iota((n_rows, 128), 1) // 32
    compact = iota((slots, 16, 128), 1) == iota((slots, 16, 128), 2) % 32

    def attend(i):
        at = slice(i * slots, i * slots + slots)
        query = qbuf[at].reshape(n_rows, 128)
        total, peaks = jnp.zeros((n_rows, 256), F32), jnp.zeros((n_rows, 128), F32)
        for g in range(4):
            scores = lax.dot_general(query, kmask[g], (((1,), (1,)), ((), ())), preferred_element_type=F32)
            scores = jnp.where(same_half, scores * 32 ** (-0.5), -1e30)
            peak = jnp.max(scores, axis=1, keepdims=True)
            total = total + dot(jnp.exp(scores - peak).astype(BF), vmask[g])
            peaks = jnp.where(group == g, peak, peaks)
        weight = total[:, 128:256]
        osend[at] = (total[:, 0:128] / weight).astype(BF).reshape(slots, 16, 128)
        level = (peaks + jnp.log(weight)).reshape(slots, 16, 128)
        lsend[at] = jnp.sum(jnp.where(compact, level, 0.0), axis=1, keepdims=True)

    others = pl.ds(1, n_row - 1)
    n_blocks = n_row // slots
    for block in sorted(range(n_blocks), key=lambda k: -min(k, n_blocks - k)):
        attend(block)
        for i in [i for i in row_far if i // slots == block]:
            for n, (src, dst) in enumerate(((osend, orecv), (lsend, lrecv))):
                pltpu.make_async_remote_copy(src_ref=src.at[i], dst_ref=dst.at[i], send_sem=rs.at[n], recv_sem=rr.at[n],
                                             device_id=row_peer(i, -1), device_id_type=MESH).start()
    orecv[0] = osend[0]
    lrecv[0] = lsend[0]
    arrived(enc_copies)
    pltpu.make_async_copy(orecv.at[others], orecv.at[others], rr.at[0]).wait()
    pltpu.make_async_copy(lrecv.at[others], lrecv.at[others], rr.at[1]).wait()

    levels = lrecv[...]
    share = jnp.exp(levels - jnp.max(levels, axis=0, keepdims=True))
    share = share / jnp.sum(share, axis=0, keepdims=True)
    spot = iota((n_row, 16, 128), 1) == iota((n_row, 16, 128), 2) % 32
    share = jnp.where(spot, share, 0.0).reshape(n_row * 16, 128)
    high = share.astype(BF)
    low = (share - high.astype(F32)).astype(BF)
    blocks = ((iota((256, 128), 0) % 128) // 32 == iota((256, 128), 1) // 32).astype(F32).astype(BF)
    share = dot(jnp.concatenate([high, low], axis=1), blocks).reshape(n_row, 16, 128)
    attended = jnp.sum(share * orecv[...].astype(F32), axis=0)
    attended = jnp.concatenate([attended[0:8], attended[8:16]], axis=1)
    attended = jnp.concatenate([attended, jnp.zeros_like(attended)], axis=0).astype(BF)
    mixture = tokens_s[...] + dot(attended, ow[...])[0:8]
    mixture = jnp.concatenate([mixture, jnp.zeros_like(mixture)], axis=0).astype(BF)
    r, k = iota((16, 16), 0), iota((16, 16), 1)
    twice = ((r // 8) * 4 + (r % 8) // 2 == k).astype(F32).astype(BF)
    upward = dot(dot(twice, mixture).astype(BF), uw[...])
    odd, right = row8 % 2 == 1, group8 >= 2
    for a in range(2):
        first = upward[0:8, a * 128:a * 128 + 128]
        second = upward[8:16, a * 128:a * 128 + 128]
        plane = jnp.where(right, jnp.where(odd, second, roll(second, 64, 1)), jnp.where(odd, roll(first, 64, 1), first))
        for y in range(8):
            up[a, y, 0] = plane[y:y + 1, :]
            uppad[1 + a, 1 + y, 1] = plane[y:y + 1, :]

    up_copies = []
    for n, (a, b, c) in enumerate(STEPS):
        sx = {-1: pl.ds(0, 1), 0: pl.ds(0, 2), 1: pl.ds(1, 1)}[a]
        dx = {-1: pl.ds(3, 1), 0: pl.ds(1, 2), 1: pl.ds(0, 1)}[a]
        sy = {-1: pl.ds(0, 1), 0: pl.ds(0, 8), 1: pl.ds(7, 1)}[b]
        dy = {-1: pl.ds(9, 1), 0: pl.ds(1, 8), 1: pl.ds(0, 1)}[b]
        up_copies.append(remote(up.at[sx, sy, pl.ds(0, 1)], uppad.at[dx, dy, pl.ds(1 - c, 1)], us.at[n], ur.at[n], (a, b, c)))
    start_all(up_copies)
    departed(vol_copies)
    departed(enc_copies)
    departed(up_copies)
    q_gone.wait()
    kv_gone.wait()
    pltpu.make_async_copy(orecv.at[others], orecv.at[others], rs.at[0]).wait()
    pltpu.make_async_copy(lrecv.at[others], lrecv.at[others], rs.at[1]).wait()

    group1 = iota((1, 128), 1) // 32

    def middle(plane, y):
        here = uppad[plane, y, 1]
        parts = []
        for q in range(4):
            part = jnp.where(group1 == q, here, 0.0)
            part = part + roll(part, 64, 1)
            parts.append(part + roll(part, 32, 1))
        return jnp.concatenate(parts, axis=1)

    def wide(plane, y):
        return jnp.concatenate([uppad[plane, y, 0], middle(plane, y), uppad[plane, y, 2]], axis=1)

    def side(n):
        return lambda plane, y: uppad[plane, y, n]

    def join_planes(planes, first, width, row_of):
        row = iota((8, width), 0)
        for plane in planes:
            xs = (range(0, 1), range(1, 5), range(5, 9), range(9, 10))[plane]
            for y2 in range(2):
                four = [row_of(plane, 1 + 4 * y2 + i) for i in range(4)]
                more = jnp.concatenate([jnp.where(row < 4, four[2 * i], four[2 * i + 1]) for i in range(2)], axis=0)
                for x in xs:
                    here = (x, slice(16 * y2, 16 * y2 + 16), slice(first, first + width))
                    joi[here] = (enc[here].astype(F32) + more).astype(BF)

    join_planes((1, 2), 128, 512, middle)
    lay_own(joi)
    arrived(up_copies)
    join_planes((1, 2), 0, 128, side(0))
    join_planes((1, 2), 640, 128, side(2))
    join_planes((0, 3), 0, 768, wide)
    row_rim = iota((16, 768), 0)
    for rim, full, y in ((enc_lo, joi_lo, 0), (enc_hi, joi_hi, 9)):
        planes = [wide(plane, y) for plane in range(4)]
        full[0] = (rim[0].astype(F32) + planes[0]).astype(BF)
        full[1] = (rim[1].astype(F32) + jnp.where(row_rim < 4, planes[1], planes[2])).astype(BF)
        full[2] = (rim[2].astype(F32) + planes[3]).astype(BF)

    def keep_result(x, h, value):
        out_ref[x, :, 256 * h:256 * h + 256] = value.astype(BF)

    convolve(joi, joi_lo, joi_hi, keep_result)


def on_device(sizes, volume, conv_in, conv_out, norm_gain, q_weight, kv_weight, out_weight, up_weight):
    n_row, n_col = (sizes[1] // 2) * sizes[2], sizes[0] * 2
    padded, rim, rows = (10, 32, 768), (3, 16, 768), (2, 16, 512)
    vmem = pltpu.VMEM
    scratch = [vmem((8, 32, 16, 32), BF)] + [vmem(padded, BF), vmem(rim, BF), vmem(rim, BF)] * 3 + [vmem(rows, BF)] * 2
    scratch += [vmem((864, 32), BF)] * 2 + [vmem((1, 256), F32), vmem((256, 256), BF), vmem((256, 512), BF), vmem((256, 256), BF), vmem((256, 256), BF)]
    scratch += [vmem((3, 1024, 256), BF), vmem((544, 1024), BF), vmem((3, 552, 256), F32), vmem((8, 256), F32)]
    scratch += [vmem((n_row, 16, 128), BF), vmem((n_col, 32, 128), BF), vmem((4, n_col * 16, 128), BF), vmem((4, n_col * 16, 256), BF)]
    scratch += [vmem((n_row, 16, 128), BF)] * 2 + [vmem((n_row, 1, 128), F32)] * 2
    scratch += [vmem((2, 8, 1, 1, 128), F32), vmem((4, 10, 3, 1, 128), F32)]
    dma = pltpu.SemaphoreType.DMA
    scratch += [dma((8,))] + [dma((26,))] * 6 + [dma((2,))] * 4
    result = pl.pallas_call(
        functools.partial(kernel, sizes),
        out_shape=jax.ShapeDtypeStruct((8, 32, 512), BF),
        in_specs=[pl.BlockSpec(memory_space=pltpu.HBM)] * 8,
        out_specs=pl.BlockSpec(memory_space=pltpu.VMEM),
        scratch_shapes=scratch,
        compiler_params=pltpu.CompilerParams(collective_id=0, has_side_effects=True, vmem_limit_bytes=48 * 2**20),
    )(*(pltpu.with_memory_space_constraint(a, pltpu.HBM) for a in (volume, conv_in.reshape(864, 32), conv_out.reshape(864, 32), norm_gain.reshape(1, 256), q_weight, kv_weight, out_weight, up_weight)))
    return result.reshape(8, 32, 16, 32)


def solution(mesh):
    placed = (P("gx", "gy", "gz", None), P(), P(), P(), P(), P(), P(), P())
    sizes = tuple(mesh.shape[name] for name in ("gx", "gy", "gz"))
    return jax.shard_map(
        functools.partial(on_device, sizes), mesh=mesh, in_specs=placed, out_specs=P("gx", "gy", "gz", None), check_vma=False
    )
```

```python
import functools

import jax
import jax.numpy as jnp
from jax import lax
from jax.experimental import pallas as pl
from jax.experimental.pallas import tpu as pltpu
from jax.sharding import PartitionSpec as P

BF = jnp.bfloat16
F32 = jnp.float32
MESH = pl.DeviceIdType.MESH
STEPS = [(a, b, c) for a in (-1, 0, 1) for b in (-1, 0, 1) for c in (-1, 0, 1) if (a, b, c) != (0, 0, 0)]
STEPS.sort(key=lambda step: -sum(abs(v) for v in step))


def iota(shape, dim):
    return lax.broadcasted_iota(jnp.int32, shape, dim)


def dot(left, right):
    return jnp.dot(left, right, preferred_element_type=F32)


def roll(value, shift, axis):
    return pltpu.roll(value, shift, axis)


def lane_window(c, width):
    if c == 0:
        return (0, 512), (128, 512)
    if c == 1:
        return (384, 128), (0, 128)
    return (0, 128), (640, 128)


def kernel(sizes, x_hbm, win_hbm, wout_hbm, gain_hbm, qw_hbm, kvw_hbm, ow_hbm, uw_hbm, out_ref,
           raw, vol, vol_lo, vol_hi, enc, enc_lo, enc_hi, joi, joi_lo, joi_hi, rows_v, rows_e, ends_s, ends_r,
           win, wout, gain, qw, kvw, ow, uw, taps, lhs, acc, tokens_s,
           qbuf, kvbuf, kmask, vmask, osend, orecv, lsend, lrecv, up, uppad,
           load_sem, vs, vr, es, er, us, ur, gs, gr, rs, rr):
    GX, GY, GZ = sizes
    gx, gy, gz = lax.axis_index("gx"), lax.axis_index("gy"), lax.axis_index("gz")
    n_row, n_col = (GY // 2) * GZ, GX * 2

    def at_mesh(x, y, z):
        return (x, y, z)

    row_y = [(gy + 2 * k) % GY for k in range(GY // 2)]
    row_z = [(gz + k) % GZ for k in range(GZ)]
    col_x = [(gx + k) % GX for k in range(GX)]
    col_y = [gy, gy // 2 * 2 + (gy + 1) % 2]

    def row_peer(i, sign=1):
        return at_mesh(gx, row_y[sign * (i // GZ) % (GY // 2)], row_z[sign * (i % GZ) % GZ])

    def col_peer(i):
        return at_mesh(col_x[i // 2], col_y[i % 2], gz)

    row_far = sorted(range(1, n_row), key=lambda i: -2 * min(i // GZ, GY // 2 - i // GZ) - min(i % GZ // 2, GZ // 2 - i % GZ // 2) - i % 2)
    col_far = sorted(range(1, n_col), key=lambda i: -min(i // 2, GX - i // 2))

    def inside(a, b, c):
        ok = None
        for at, step, size in ((gx, a, GX), (gy, b, GY), (gz, c, GZ)):
            if step:
                here = at < size - 1 if step > 0 else at > 0
                ok = here if ok is None else ok & here
        return ok

    def neighbour(a, b, c):
        return at_mesh(gx + a, gy + b, gz + c)

    for ref in (vol, enc):
        for x in (0, 9):
            ref[x] = jnp.zeros((32, 768), BF)
    for z in (0, 640):
        enc[1:9, :, z:z + 128] = jnp.zeros((8, 32, 128), BF)
    for ref in (ends_r, vol_lo, vol_hi, enc_lo, enc_hi, uppad):
        ref[...] = jnp.zeros(ref.shape, ref.dtype)
    barrier = pltpu.get_barrier_semaphore()
    for i in row_far:
        pl.semaphore_signal(barrier, inc=1, device_id=row_peer(i), device_id_type=MESH)
    for i in col_far:
        pl.semaphore_signal(barrier, inc=1, device_id=col_peer(i), device_id_type=MESH)
    for step in STEPS:
        @pl.when(inside(*step))
        def _(step=step):
            pl.semaphore_signal(barrier, inc=1, device_id=neighbour(*step), device_id_type=MESH)

    own = (pl.ds(1, 8), pl.ds(0, 32), pl.ds(128, 512))
    loads = [pltpu.make_async_copy(x_hbm, raw, load_sem.at[0])]
    pairs = [(win_hbm, win), (wout_hbm, wout), (gain_hbm, gain), (qw_hbm, qw), (kvw_hbm, kvw), (ow_hbm, ow), (uw_hbm, uw)]
    loads += [pltpu.make_async_copy(s, d, load_sem.at[i + 1]) for i, (s, d) in enumerate(pairs)]
    for copy in loads:
        copy.start()

    def pack_rows(main, rows):
        r, k = iota((32, 256), 0), iota((32, 256), 1)
        wanted = jnp.where(r < 16, r * 32, (r - 16) * 32 + 31)
        picked = dot((wanted == k).astype(F32).astype(BF), main[own].reshape(256, 512))
        rows[...] = picked.astype(BF).reshape(2, 16, 512)

    def remote(src, dst, send, recv, step):
        copy = pltpu.make_async_remote_copy(src_ref=src, dst_ref=dst, send_sem=send, recv_sem=recv,
                                            device_id=neighbour(*step), device_id_type=MESH)
        return copy, pltpu.make_async_copy(dst, dst, recv), pltpu.make_async_copy(src, src, send)

    def turn(value, groups):
        return roll(value, 32 * groups % 128, 1) if groups % 4 else value

    def pack_ends(main):
        group = iota((32, 128), 1) // 32
        for n, (first, at) in enumerate(((128, 0), (512, 3))):
            for p in range(2):
                planes = [jnp.where(group == at, main[1 + 2 * g + p, :, first:first + 128].astype(F32), 0.0) for g in range(4)]
                ends_s[n, p] = sum(turn(v, g - at) for g, v in enumerate(planes)).astype(BF)

    def unpack_ends(main):
        for n, (first, at) in enumerate(((640, 0), (0, 3))):
            for p in range(2):
                value = ends_r[n, p].astype(F32)
                for g in range(4):
                    main[1 + 2 * g + p, :, first:first + 128] = turn(value, at - g).astype(BF)

    def halo_copies(main, rows, lo, hi, send, recv, packed=False):
        copies = []
        for n, (a, b, c) in enumerate(STEPS):
            (s0, width), (d0, _) = lane_window(c, 512)
            if packed and a == 0 and b == 0:
                src, dst = ends_s.at[(c + 1) // 2], ends_r.at[(c + 1) // 2]
            elif b == 0:
                sx = {-1: pl.ds(1, 1), 0: pl.ds(1, 8), 1: pl.ds(8, 1)}[a]
                dx = {-1: pl.ds(9, 1), 0: pl.ds(1, 8), 1: pl.ds(0, 1)}[a]
                src = main.at[sx, pl.ds(0, 32), pl.ds(128 + s0, width)]
                dst = main.at[dx, pl.ds(0, 32), pl.ds(d0, width)]
            else:
                src = rows.at[1 if b == 1 else 0, pl.ds(0, 16), pl.ds(s0, width)]
                dst = (lo if b == 1 else hi).at[1 - a, pl.ds(0, 16), pl.ds(d0, width)]
            copies.append(remote(src, dst, send.at[n], recv.at[n], (a, b, c)))
        return copies

    def start_all(copies):
        for step, (copy, _, _) in zip(STEPS, copies):
            @pl.when(inside(*step))
            def _(copy=copy):
                copy.start()

    def arrived(copies):
        for (a, b, c), (_, landing, _) in zip(STEPS, copies):
            @pl.when(inside(-a, -b, -c))
            def _(landing=landing):
                landing.wait()

    def departed(copies):
        for step, (_, _, leaving) in zip(STEPS, copies):
            @pl.when(inside(*step))
            def _(leaving=leaving):
                leaving.wait()

    def spread_taps(w):
        k, n = iota((32, 512), 0), iota((32, 512), 1)
        place = ((n % 32 == k) & (n // 128 == (n % 128) // 32)).astype(F32).astype(BF)
        moved = dot(w[...], place).astype(BF)
        taps[...] = jnp.zeros(taps.shape, BF)
        for dx in range(3):
            for dy in range(3):
                first = (dx * 3 + dy) * 96
                for m in range(2):
                    for z in range(8):
                        total = None
                        for g in range(4):
                            dz = z - 4 * m - g + 1
                            if 0 <= dz <= 2:
                                piece = moved[first + dz * 32:first + dz * 32 + 32, g * 128:g * 128 + 128]
                                total = piece if total is None else total + piece
                        if total is not None:
                            r0 = dx * 256 + z * 32
                            taps[dy, r0:r0 + 32, m * 128:m * 128 + 128] = total
                above, below = 768 + 32 * (0, 2, 4)[dx], 768 + 32 * (3, 1, 7)[dx]
                taps[dy, above:above + 32, 128:256] = moved[first + 64:first + 96, 384:512]
                taps[dy, below:below + 32, 0:128] = moved[first:first + 32, 0:128]

    def lay_own(main):
        for h in range(2):
            o = 128 + 256 * h
            for dx, x0, x1 in ((0, 1, 8), (1, 0, 8), (2, 0, 7)):
                planes = main[x0 + dx:x1 + dx, :, o:o + 256].reshape((x1 - x0) * 32, 256)
                lhs[h * 256 + 32 * x0:h * 256 + 32 * x1, dx * 256:dx * 256 + 256] = planes

    def convolve(main, lo, hi, emit):
        row8 = iota((8, 768), 0)

        def three(rim):
            before, here, after = (rim[i].astype(F32)[0:8] for i in range(3))
            return (jnp.where(row8 == 0, roll(before, 1, 0), roll(here, 1, 0)), here,
                    jnp.where(row8 == 7, roll(after, 7, 0), roll(here, 7, 0)))

        rims = [jnp.concatenate(p, axis=0) for p in zip(three(lo), three(hi))]
        g = iota((1, 128), 1) // 32
        last, first = (g == 3).astype(F32), (g == 0).astype(F32)
        for h, (a, b) in enumerate(((0, 384), (256, 640))):
            rows, few = slice(h * 256, h * 256 + 256), slice(512 + 16 * h, 528 + 16 * h)
            o = 128 + 256 * h
            for dx in range(3):
                if dx != 1:
                    edge, plane = (h * 256, 0) if dx == 0 else (h * 256 + 224, 9)
                    lhs[edge:edge + 32, dx * 256:dx * 256 + 256] = main[plane, :, o:o + 256]
                lhs[few, dx * 256:dx * 256 + 256] = rims[dx][:, o:o + 256].astype(BF)
            ends = (main[:, :, a:a + 128].reshape(320, 128) * last.astype(BF) + main[:, :, b:b + 128].reshape(320, 128) * first.astype(BF))
            turned = roll(ends[32:288].astype(F32), 64, 1).astype(BF)
            lhs[rows, 768:896] = ends[0:256] + turned
            lhs[rows, 896:1024] = ends[64:320]
            ends = [rim[:, a:a + 128] * last + rim[:, b:b + 128] * first for rim in rims]
            lhs[few, 768:896] = (ends[0] + roll(ends[1], 64, 1)).astype(BF)
            lhs[few, 896:1024] = ends[2].astype(BF)

        def one(dy, carry):
            acc[dy, 0:544, :] = dot(lhs[...], taps[dy])
            return carry

        lax.fori_loop(0, 3, one, 0)
        row = iota((32, 256), 0)

        def join(x, carry):
            for h in range(2):
                at = pl.ds(pl.multiple_of(h * 256 + x * 32, 32), 32)
                below = jnp.where(row == 0, acc[0, pl.ds(512 + 16 * h + x, 1), :], roll(acc[0, at, :], 1, 0))
                above = jnp.where(row == 31, acc[2, pl.ds(520 + 16 * h + x, 1), :], roll(acc[2, at, :], 31, 0))
                emit(x, h, below + acc[1, at, :] + above)
            return carry

        lax.fori_loop(0, 8, join, 0)

    loads[0].wait()
    for x in range(8):
        vol[1 + x, :, 128:640] = raw[x].reshape(32, 512)
    pack_rows(vol, rows_v)
    pack_ends(vol)
    neighbours = (1 + (gx > 0).astype(jnp.int32) + (gx < GX - 1).astype(jnp.int32))
    neighbours *= (1 + (gy > 0).astype(jnp.int32) + (gy < GY - 1).astype(jnp.int32))
    neighbours *= (1 + (gz > 0).astype(jnp.int32) + (gz < GZ - 1).astype(jnp.int32))
    pl.semaphore_wait(barrier, neighbours - 1 + n_row - 1 + n_col - 1)
    vol_copies = halo_copies(vol, rows_v, vol_lo, vol_hi, vs, vr, True)
    start_all(vol_copies)
    for copy in loads[1:]:
        copy.wait()
    lay_own(vol)
    spread_taps(win)
    arrived(vol_copies)
    unpack_ends(vol)

    def keep_encoded(x, h, value):
        enc[1 + x, :, 128 + 256 * h:384 + 256 * h] = jnp.maximum(value, 0.0).astype(BF)

    convolve(vol, vol_lo, vol_hi, keep_encoded)

    r, k = iota((32, 256), 0), iota((32, 256), 1)
    pool = ((k // 128 == r // 16) & ((k % 32) // 4 == 2 * (r % 4) + (r // 8) % 2)).astype(F32).astype(BF)
    sums = dot(pool, enc[own].reshape(256, 512))
    row8, group8 = iota((8, 128), 0), iota((8, 128), 1) // 32
    chunks = []
    for q in range(4):
        part = sums[:, q * 128:q * 128 + 128]
        part = part + roll(part, 64, 1)
        chunks.append(part + roll(part, 32, 1))

    def cell(ab, c):
        return jnp.where(row8 < 4, chunks[c][ab * 8:ab * 8 + 8], chunks[2 + c][ab * 8:ab * 8 + 8])

    sides = []
    for a in range(2):
        side = cell(2 * a + 1, 1)
        for n, (b, c) in enumerate(((0, 0), (0, 1), (1, 0))):
            side = jnp.where(group8 == n, cell(2 * a + b, c), side)
        sides.append(side)
    tokens = jnp.concatenate(sides, axis=1) * (1.0 / 64.0)
    tokens_s[...] = tokens
    center = tokens - jnp.mean(tokens, axis=1, keepdims=True)
    variance = jnp.mean(center * center, axis=1, keepdims=True)
    normed = center * lax.rsqrt(variance + 1e-05) * gain[...]
    normed = jnp.concatenate([normed, jnp.zeros_like(normed)], axis=0).astype(BF)
    queries = dot(normed, qw[...])[0:8]
    key_value = dot(normed, kvw[...])[0:8]
    qbuf[0] = jnp.concatenate([queries[:, i * 128:i * 128 + 128] for i in range(2)], axis=0).astype(BF)
    kvbuf[0] = jnp.concatenate([key_value[:, i * 128:i * 128 + 128] for i in range(4)], axis=0).astype(BF)

    q_all = pltpu.make_async_copy(qbuf.at[pl.ds(1, n_row - 1)], qbuf.at[pl.ds(1, n_row - 1)], gr.at[0])
    kv_all = pltpu.make_async_copy(kvbuf.at[pl.ds(1, n_col - 1)], kvbuf.at[pl.ds(1, n_col - 1)], gr.at[1])
    q_gone = pltpu.make_async_copy(qbuf.at[pl.ds(1, n_row - 1)], qbuf.at[pl.ds(1, n_row - 1)], gs.at[0])
    kv_gone = pltpu.make_async_copy(kvbuf.at[pl.ds(1, n_col - 1)], kvbuf.at[pl.ds(1, n_col - 1)], gs.at[1])
    sends = [(n / len(row_far), qbuf, 0, i, row_peer(i)) for n, i in enumerate(row_far)]
    sends += [(n / len(col_far), kvbuf, 1, i, col_peer(i)) for n, i in enumerate(col_far)]
    for _, buf, n, i, peer in sorted(sends, key=lambda s: s[0]):
        pltpu.make_async_remote_copy(src_ref=buf.at[0], dst_ref=buf.at[i], send_sem=gs.at[n], recv_sem=gr.at[n],
                                     device_id=peer, device_id_type=MESH).start()
    pack_rows(enc, rows_e)
    enc_copies = halo_copies(enc, rows_e, enc_lo, enc_hi, es, er)
    start_all(enc_copies)
    spread_taps(wout)

    q_all.wait()
    kv_all.wait()
    n_keys = n_col * 16
    lane_group = iota((n_keys, 128), 1) // 32
    keys = kvbuf[:, 0:16, :].reshape(n_keys, 128)
    values = kvbuf[:, 16:32, :].reshape(n_keys, 128)
    for g in range(4):
        mine = (lane_group == g).astype(F32).astype(BF)
        kmask[g] = keys * mine
        vmask[g, :, 0:128] = values * mine
        vmask[g, :, 128:256] = mine
    slots = min(8, n_row)
    n_rows = slots * 16
    same_half = (iota((n_rows, n_keys), 0) // 8) % 2 == (iota((n_rows, n_keys), 1) // 8) % 2
    group = iota((n_rows, 128), 1) // 32
    compact = iota((slots, 16, 128), 1) == iota((slots, 16, 128), 2) % 32

    def attend(i):
        at = slice(i * slots, i * slots + slots)
        query = qbuf[at].reshape(n_rows, 128)
        total, peaks = jnp.zeros((n_rows, 256), F32), jnp.zeros((n_rows, 128), F32)
        for g in range(4):
            scores = lax.dot_general(query, kmask[g], (((1,), (1,)), ((), ())), preferred_element_type=F32)
            scores = jnp.where(same_half, scores * 32 ** (-0.5), -1e30)
            peak = jnp.max(scores, axis=1, keepdims=True)
            total = total + dot(jnp.exp(scores - peak).astype(BF), vmask[g])
            peaks = jnp.where(group == g, peak, peaks)
        weight = total[:, 128:256]
        osend[at] = (total[:, 0:128] / weight).astype(BF).reshape(slots, 16, 128)
        level = (peaks + jnp.log(weight)).reshape(slots, 16, 128)
        lsend[at] = jnp.sum(jnp.where(compact, level, 0.0), axis=1, keepdims=True)

    others = pl.ds(1, n_row - 1)
    n_blocks = n_row // slots
    for block in sorted(range(n_blocks), key=lambda k: -min(k, n_blocks - k)):
        attend(block)
        for i in [i for i in row_far if i // slots == block]:
            for n, (src, dst) in enumerate(((osend, orecv), (lsend, lrecv))):
                pltpu.make_async_remote_copy(src_ref=src.at[i], dst_ref=dst.at[i], send_sem=rs.at[n], recv_sem=rr.at[n],
                                             device_id=row_peer(i, -1), device_id_type=MESH).start()
    orecv[0] = osend[0]
    lrecv[0] = lsend[0]
    arrived(enc_copies)
    pltpu.make_async_copy(orecv.at[others], orecv.at[others], rr.at[0]).wait()
    pltpu.make_async_copy(lrecv.at[others], lrecv.at[others], rr.at[1]).wait()

    levels = lrecv[...]
    share = jnp.exp(levels - jnp.max(levels, axis=0, keepdims=True))
    share = share / jnp.sum(share, axis=0, keepdims=True)
    spot = iota((n_row, 16, 128), 1) == iota((n_row, 16, 128), 2) % 32
    share = jnp.where(spot, share, 0.0).reshape(n_row * 16, 128)
    high = share.astype(BF)
    low = (share - high.astype(F32)).astype(BF)
    blocks = ((iota((256, 128), 0) % 128) // 32 == iota((256, 128), 1) // 32).astype(F32).astype(BF)
    share = dot(jnp.concatenate([high, low], axis=1), blocks).reshape(n_row, 16, 128)
    attended = jnp.sum(share * orecv[...].astype(F32), axis=0)
    attended = jnp.concatenate([attended[0:8], attended[8:16]], axis=1)
    attended = jnp.concatenate([attended, jnp.zeros_like(attended)], axis=0).astype(BF)
    mixture = tokens_s[...] + dot(attended, ow[...])[0:8]
    mixture = jnp.concatenate([mixture, jnp.zeros_like(mixture)], axis=0).astype(BF)
    r, k = iota((16, 16), 0), iota((16, 16), 1)
    twice = ((r // 8) * 4 + (r % 8) // 2 == k).astype(F32).astype(BF)
    upward = dot(dot(twice, mixture).astype(BF), uw[...])
    odd, right = row8 % 2 == 1, group8 >= 2
    for a in range(2):
        first = upward[0:8, a * 128:a * 128 + 128]
        second = upward[8:16, a * 128:a * 128 + 128]
        plane = jnp.where(right, jnp.where(odd, second, roll(second, 64, 1)), jnp.where(odd, roll(first, 64, 1), first))
        for y in range(8):
            up[a, y, 0] = plane[y:y + 1, :]
            uppad[1 + a, 1 + y, 1] = plane[y:y + 1, :]

    up_copies = []
    for n, (a, b, c) in enumerate(STEPS):
        sx = {-1: pl.ds(0, 1), 0: pl.ds(0, 2), 1: pl.ds(1, 1)}[a]
        dx = {-1: pl.ds(3, 1), 0: pl.ds(1, 2), 1: pl.ds(0, 1)}[a]
        sy = {-1: pl.ds(0, 1), 0: pl.ds(0, 8), 1: pl.ds(7, 1)}[b]
        dy = {-1: pl.ds(9, 1), 0: pl.ds(1, 8), 1: pl.ds(0, 1)}[b]
        up_copies.append(remote(up.at[sx, sy, pl.ds(0, 1)], uppad.at[dx, dy, pl.ds(1 - c, 1)], us.at[n], ur.at[n], (a, b, c)))
    start_all(up_copies)
    departed(vol_copies)
    departed(enc_copies)
    departed(up_copies)
    q_gone.wait()
    kv_gone.wait()
    pltpu.make_async_copy(orecv.at[others], orecv.at[others], rs.at[0]).wait()
    pltpu.make_async_copy(lrecv.at[others], lrecv.at[others], rs.at[1]).wait()

    group1 = iota((1, 128), 1) // 32

    def middle(plane, y):
        here = uppad[plane, y, 1]
        parts = []
        for q in range(4):
            part = jnp.where(group1 == q, here, 0.0)
            part = part + roll(part, 64, 1)
            parts.append(part + roll(part, 32, 1))
        return jnp.concatenate(parts, axis=1)

    def wide(plane, y):
        return jnp.concatenate([uppad[plane, y, 0], middle(plane, y), uppad[plane, y, 2]], axis=1)

    def side(n):
        return lambda plane, y: uppad[plane, y, n]

    def join_planes(planes, first, width, row_of):
        row = iota((8, width), 0)
        for plane in planes:
            xs = (range(0, 1), range(1, 5), range(5, 9), range(9, 10))[plane]
            for y2 in range(2):
                four = [row_of(plane, 1 + 4 * y2 + i) for i in range(4)]
                more = jnp.concatenate([jnp.where(row < 4, four[2 * i], four[2 * i + 1]) for i in range(2)], axis=0)
                for x in xs:
                    here = (x, slice(16 * y2, 16 * y2 + 16), slice(first, first + width))
                    joi[here] = (enc[here].astype(F32) + more).astype(BF)

    join_planes((1, 2), 128, 512, middle)
    lay_own(joi)
    arrived(up_copies)
    join_planes((1, 2), 0, 128, side(0))
    join_planes((1, 2), 640, 128, side(2))
    join_planes((0, 3), 0, 768, wide)
    row_rim = iota((16, 768), 0)
    for rim, full, y in ((enc_lo, joi_lo, 0), (enc_hi, joi_hi, 9)):
        planes = [wide(plane, y) for plane in range(4)]
        full[0] = (rim[0].astype(F32) + planes[0]).astype(BF)
        full[1] = (rim[1].astype(F32) + jnp.where(row_rim < 4, planes[1], planes[2])).astype(BF)
        full[2] = (rim[2].astype(F32) + planes[3]).astype(BF)

    def keep_result(x, h, value):
        out_ref[x, :, 256 * h:256 * h + 256] = value.astype(BF)

    convolve(joi, joi_lo, joi_hi, keep_result)


def on_device(sizes, volume, conv_in, conv_out, norm_gain, q_weight, kv_weight, out_weight, up_weight):
    n_row, n_col = (sizes[1] // 2) * sizes[2], sizes[0] * 2
    padded, rim, rows = (10, 32, 768), (3, 16, 768), (2, 16, 512)
    vmem = pltpu.VMEM
    scratch = [vmem((8, 32, 16, 32), BF)] + [vmem(padded, BF), vmem(rim, BF), vmem(rim, BF)] * 3 + [vmem(rows, BF)] * 2 + [vmem((2, 2, 32, 128), BF)] * 2
    scratch += [vmem((864, 32), BF)] * 2 + [vmem((1, 256), F32), vmem((256, 256), BF), vmem((256, 512), BF), vmem((256, 256), BF), vmem((256, 256), BF)]
    scratch += [vmem((3, 1024, 256), BF), vmem((544, 1024), BF), vmem((3, 552, 256), F32), vmem((8, 256), F32)]
    scratch += [vmem((n_row, 16, 128), BF), vmem((n_col, 32, 128), BF), vmem((4, n_col * 16, 128), BF), vmem((4, n_col * 16, 256), BF)]
    scratch += [vmem((n_row, 16, 128), BF)] * 2 + [vmem((n_row, 1, 128), F32)] * 2
    scratch += [vmem((2, 8, 1, 1, 128), F32), vmem((4, 10, 3, 1, 128), F32)]
    dma = pltpu.SemaphoreType.DMA
    scratch += [dma((8,))] + [dma((26,))] * 6 + [dma((2,))] * 4
    result = pl.pallas_call(
        functools.partial(kernel, sizes),
        out_shape=jax.ShapeDtypeStruct((8, 32, 512), BF),
        in_specs=[pl.BlockSpec(memory_space=pltpu.HBM)] * 8,
        out_specs=pl.BlockSpec(memory_space=pltpu.VMEM),
        scratch_shapes=scratch,
        compiler_params=pltpu.CompilerParams(collective_id=0, has_side_effects=True, vmem_limit_bytes=48 * 2**20),
    )(*(pltpu.with_memory_space_constraint(a, pltpu.HBM) for a in (volume, conv_in.reshape(864, 32), conv_out.reshape(864, 32), norm_gain.reshape(1, 256), q_weight, kv_weight, out_weight, up_weight)))
    return result.reshape(8, 32, 16, 32)


def solution(mesh):
    placed = (P("gx", "gy", "gz", None), P(), P(), P(), P(), P(), P(), P())
    sizes = tuple(mesh.shape[name] for name in ("gx", "gy", "gz"))
    return jax.shard_map(
        functools.partial(on_device, sizes), mesh=mesh, in_specs=placed, out_specs=P("gx", "gy", "gz", None), check_vma=False
    )
```

```python
import functools

import jax
import jax.numpy as jnp
from jax import lax
from jax.experimental import pallas as pl
from jax.experimental.pallas import tpu as pltpu
from jax.sharding import PartitionSpec as P

BF = jnp.bfloat16
F32 = jnp.float32
MESH = pl.DeviceIdType.MESH
STEPS = [(a, b, c) for a in (-1, 0, 1) for b in (-1, 0, 1) for c in (-1, 0, 1) if (a, b, c) != (0, 0, 0)]
STEPS.sort(key=lambda step: -sum(abs(v) for v in step))


def iota(shape, dim):
    return lax.broadcasted_iota(jnp.int32, shape, dim)


def dot(left, right):
    return jnp.dot(left, right, preferred_element_type=F32)


def roll(value, shift, axis):
    return pltpu.roll(value, shift, axis)


def lane_window(c, width):
    if c == 0:
        return (0, 512), (128, 512)
    if c == 1:
        return (384, 128), (0, 128)
    return (0, 128), (640, 128)


def kernel(sizes, x_hbm, win_hbm, wout_hbm, gain_hbm, qw_hbm, kvw_hbm, ow_hbm, uw_hbm, out_ref,
           raw, vol, vol_lo, vol_hi, enc, enc_lo, enc_hi, joi, joi_lo, joi_hi, rows_v, rows_e, ends_s, ends_r, enc_s, enc_r,
           win, wout, gain, qw, kvw, ow, uw, taps, lhs, acc, tokens_s,
           qbuf, kvbuf, kmask, vmask, osend, orecv, lsend, lrecv, up, uppad,
           load_sem, vs, vr, es, er, us, ur, gs, gr, rs, rr):
    GX, GY, GZ = sizes
    gx, gy, gz = lax.axis_index("gx"), lax.axis_index("gy"), lax.axis_index("gz")
    n_row, n_col = (GY // 2) * GZ, GX * 2

    def at_mesh(x, y, z):
        return (x, y, z)

    row_y = [(gy + 2 * k) % GY for k in range(GY // 2)]
    row_z = [(gz + k) % GZ for k in range(GZ)]
    col_x = [(gx + k) % GX for k in range(GX)]
    col_y = [gy, gy // 2 * 2 + (gy + 1) % 2]

    def row_peer(i, sign=1):
        return at_mesh(gx, row_y[sign * (i // GZ) % (GY // 2)], row_z[sign * (i % GZ) % GZ])

    def col_peer(i):
        return at_mesh(col_x[i // 2], col_y[i % 2], gz)

    row_far = sorted(range(1, n_row), key=lambda i: -2 * min(i // GZ, GY // 2 - i // GZ) - min(i % GZ // 2, GZ // 2 - i % GZ // 2) - i % 2)
    col_far = sorted(range(1, n_col), key=lambda i: -min(i // 2, GX - i // 2))

    def inside(a, b, c):
        ok = None
        for at, step, size in ((gx, a, GX), (gy, b, GY), (gz, c, GZ)):
            if step:
                here = at < size - 1 if step > 0 else at > 0
                ok = here if ok is None else ok & here
        return ok

    def neighbour(a, b, c):
        return at_mesh(gx + a, gy + b, gz + c)

    for ref in (vol, enc):
        for x in (0, 9):
            ref[x] = jnp.zeros((32, 768), BF)
    for ref in (ends_r, enc_r, vol_lo, vol_hi, enc_lo, enc_hi, uppad):
        ref[...] = jnp.zeros(ref.shape, ref.dtype)
    barrier = pltpu.get_barrier_semaphore()
    for i in row_far:
        pl.semaphore_signal(barrier, inc=1, device_id=row_peer(i), device_id_type=MESH)
    for i in col_far:
        pl.semaphore_signal(barrier, inc=1, device_id=col_peer(i), device_id_type=MESH)
    for step in STEPS:
        @pl.when(inside(*step))
        def _(step=step):
            pl.semaphore_signal(barrier, inc=1, device_id=neighbour(*step), device_id_type=MESH)

    own = (pl.ds(1, 8), pl.ds(0, 32), pl.ds(128, 512))
    loads = [pltpu.make_async_copy(x_hbm, raw, load_sem.at[0])]
    pairs = [(win_hbm, win), (wout_hbm, wout), (gain_hbm, gain), (qw_hbm, qw), (kvw_hbm, kvw), (ow_hbm, ow), (uw_hbm, uw)]
    loads += [pltpu.make_async_copy(s, d, load_sem.at[i + 1]) for i, (s, d) in enumerate(pairs)]
    for copy in loads:
        copy.start()

    def pack_rows(main, rows):
        r, k = iota((32, 256), 0), iota((32, 256), 1)
        wanted = jnp.where(r < 16, r * 32, (r - 16) * 32 + 31)
        picked = dot((wanted == k).astype(F32).astype(BF), main[own].reshape(256, 512))
        rows[...] = picked.astype(BF).reshape(2, 16, 512)

    def remote(src, dst, send, recv, step):
        copy = pltpu.make_async_remote_copy(src_ref=src, dst_ref=dst, send_sem=send, recv_sem=recv,
                                            device_id=neighbour(*step), device_id_type=MESH)
        return copy, pltpu.make_async_copy(dst, dst, recv), pltpu.make_async_copy(src, src, send)

    def turn(value, groups):
        return roll(value, 32 * groups % 128, 1) if groups % 4 else value

    def pack_ends(main, out):
        group = iota((32, 128), 1) // 32
        for n, (first, at) in enumerate(((128, 0), (512, 3))):
            for p in range(2):
                planes = [jnp.where(group == at, main[1 + 2 * g + p, :, first:first + 128].astype(F32), 0.0) for g in range(4)]
                out[n, p] = sum(turn(v, g - at) for g, v in enumerate(planes)).astype(BF)

    def unpack_ends(main, into):
        for n, (first, at) in enumerate(((640, 0), (0, 3))):
            for p in range(2):
                value = into[n, p].astype(F32)
                for g in range(4):
                    main[1 + 2 * g + p, :, first:first + 128] = turn(value, at - g).astype(BF)

    def halo_copies(main, rows, lo, hi, send, recv, out, into):
        copies = []
        for n, (a, b, c) in enumerate(STEPS):
            (s0, width), (d0, _) = lane_window(c, 512)
            if a == 0 and b == 0:
                src, dst = out.at[(c + 1) // 2], into.at[(c + 1) // 2]
            elif b == 0:
                sx = {-1: pl.ds(1, 1), 0: pl.ds(1, 8), 1: pl.ds(8, 1)}[a]
                dx = {-1: pl.ds(9, 1), 0: pl.ds(1, 8), 1: pl.ds(0, 1)}[a]
                src = main.at[sx, pl.ds(0, 32), pl.ds(128 + s0, width)]
                dst = main.at[dx, pl.ds(0, 32), pl.ds(d0, width)]
            else:
                src = rows.at[1 if b == 1 else 0, pl.ds(0, 16), pl.ds(s0, width)]
                dst = (lo if b == 1 else hi).at[1 - a, pl.ds(0, 16), pl.ds(d0, width)]
            copies.append(remote(src, dst, send.at[n], recv.at[n], (a, b, c)))
        return copies

    def start_all(copies):
        for step, (copy, _, _) in zip(STEPS, copies):
            @pl.when(inside(*step))
            def _(copy=copy):
                copy.start()

    def arrived(copies):
        for (a, b, c), (_, landing, _) in zip(STEPS, copies):
            @pl.when(inside(-a, -b, -c))
            def _(landing=landing):
                landing.wait()

    def departed(copies):
        for step, (_, _, leaving) in zip(STEPS, copies):
            @pl.when(inside(*step))
            def _(leaving=leaving):
                leaving.wait()

    def spread_taps(w):
        k, n = iota((32, 512), 0), iota((32, 512), 1)
        place = ((n % 32 == k) & (n // 128 == (n % 128) // 32)).astype(F32).astype(BF)
        moved = dot(w[...], place).astype(BF)
        taps[...] = jnp.zeros(taps.shape, BF)
        for dx in range(3):
            for dy in range(3):
                first = (dx * 3 + dy) * 96
                for m in range(2):
                    for z in range(8):
                        total = None
                        for g in range(4):
                            dz = z - 4 * m - g + 1
                            if 0 <= dz <= 2:
                                piece = moved[first + dz * 32:first + dz * 32 + 32, g * 128:g * 128 + 128]
                                total = piece if total is None else total + piece
                        if total is not None:
                            r0 = dx * 256 + z * 32
                            taps[dy, r0:r0 + 32, m * 128:m * 128 + 128] = total
                above, below = 768 + 32 * (0, 2, 4)[dx], 768 + 32 * (3, 1, 7)[dx]
                taps[dy, above:above + 32, 128:256] = moved[first + 64:first + 96, 384:512]
                taps[dy, below:below + 32, 0:128] = moved[first:first + 32, 0:128]

    def lay_own(main):
        for h in range(2):
            o = 128 + 256 * h
            for dx, x0, x1 in ((0, 1, 8), (1, 0, 8), (2, 0, 7)):
                planes = main[x0 + dx:x1 + dx, :, o:o + 256].reshape((x1 - x0) * 32, 256)
                lhs[h * 256 + 32 * x0:h * 256 + 32 * x1, dx * 256:dx * 256 + 256] = planes

    def convolve(main, lo, hi, emit):
        row8 = iota((8, 768), 0)

        def three(rim):
            before, here, after = (rim[i].astype(F32)[0:8] for i in range(3))
            return (jnp.where(row8 == 0, roll(before, 1, 0), roll(here, 1, 0)), here,
                    jnp.where(row8 == 7, roll(after, 7, 0), roll(here, 7, 0)))

        rims = [jnp.concatenate(p, axis=0) for p in zip(three(lo), three(hi))]
        g = iota((1, 128), 1) // 32
        last, first = (g == 3).astype(F32), (g == 0).astype(F32)
        for h, (a, b) in enumerate(((0, 384), (256, 640))):
            rows, few = slice(h * 256, h * 256 + 256), slice(512 + 16 * h, 528 + 16 * h)
            o = 128 + 256 * h
            for dx in range(3):
                if dx != 1:
                    edge, plane = (h * 256, 0) if dx == 0 else (h * 256 + 224, 9)
                    lhs[edge:edge + 32, dx * 256:dx * 256 + 256] = main[plane, :, o:o + 256]
                lhs[few, dx * 256:dx * 256 + 256] = rims[dx][:, o:o + 256].astype(BF)
            ends = (main[:, :, a:a + 128].reshape(320, 128) * last.astype(BF) + main[:, :, b:b + 128].reshape(320, 128) * first.astype(BF))
            turned = roll(ends[32:288].astype(F32), 64, 1).astype(BF)
            lhs[rows, 768:896] = ends[0:256] + turned
            lhs[rows, 896:1024] = ends[64:320]
            ends = [rim[:, a:a + 128] * last + rim[:, b:b + 128] * first for rim in rims]
            lhs[few, 768:896] = (ends[0] + roll(ends[1], 64, 1)).astype(BF)
            lhs[few, 896:1024] = ends[2].astype(BF)

        def one(dy, carry):
            acc[dy, 0:544, :] = dot(lhs[...], taps[dy])
            return carry

        lax.fori_loop(0, 3, one, 0)
        row = iota((32, 256), 0)

        def join(x, carry):
            for h in range(2):
                at = pl.ds(pl.multiple_of(h * 256 + x * 32, 32), 32)
                below = jnp.where(row == 0, acc[0, pl.ds(512 + 16 * h + x, 1), :], roll(acc[0, at, :], 1, 0))
                above = jnp.where(row == 31, acc[2, pl.ds(520 + 16 * h + x, 1), :], roll(acc[2, at, :], 31, 0))
                emit(x, h, below + acc[1, at, :] + above)
            return carry

        lax.fori_loop(0, 8, join, 0)

    loads[0].wait()
    for x in range(8):
        vol[1 + x, :, 128:640] = raw[x].reshape(32, 512)
    pack_rows(vol, rows_v)
    pack_ends(vol, ends_s)
    neighbours = (1 + (gx > 0).astype(jnp.int32) + (gx < GX - 1).astype(jnp.int32))
    neighbours *= (1 + (gy > 0).astype(jnp.int32) + (gy < GY - 1).astype(jnp.int32))
    neighbours *= (1 + (gz > 0).astype(jnp.int32) + (gz < GZ - 1).astype(jnp.int32))
    pl.semaphore_wait(barrier, neighbours - 1 + n_row - 1 + n_col - 1)
    vol_copies = halo_copies(vol, rows_v, vol_lo, vol_hi, vs, vr, ends_s, ends_r)
    start_all(vol_copies)
    for copy in loads[1:]:
        copy.wait()
    lay_own(vol)
    spread_taps(win)
    arrived(vol_copies)
    unpack_ends(vol, ends_r)

    def keep_encoded(x, h, value):
        enc[1 + x, :, 128 + 256 * h:384 + 256 * h] = jnp.maximum(value, 0.0).astype(BF)

    convolve(vol, vol_lo, vol_hi, keep_encoded)

    r, k = iota((32, 256), 0), iota((32, 256), 1)
    pool = ((k // 128 == r // 16) & ((k % 32) // 4 == 2 * (r % 4) + (r // 8) % 2)).astype(F32).astype(BF)
    sums = dot(pool, enc[own].reshape(256, 512))
    row8, group8 = iota((8, 128), 0), iota((8, 128), 1) // 32
    chunks = []
    for q in range(4):
        part = sums[:, q * 128:q * 128 + 128]
        part = part + roll(part, 64, 1)
        chunks.append(part + roll(part, 32, 1))

    def cell(ab, c):
        return jnp.where(row8 < 4, chunks[c][ab * 8:ab * 8 + 8], chunks[2 + c][ab * 8:ab * 8 + 8])

    sides = []
    for a in range(2):
        side = cell(2 * a + 1, 1)
        for n, (b, c) in enumerate(((0, 0), (0, 1), (1, 0))):
            side = jnp.where(group8 == n, cell(2 * a + b, c), side)
        sides.append(side)
    tokens = jnp.concatenate(sides, axis=1) * (1.0 / 64.0)
    tokens_s[...] = tokens
    center = tokens - jnp.mean(tokens, axis=1, keepdims=True)
    variance = jnp.mean(center * center, axis=1, keepdims=True)
    normed = center * lax.rsqrt(variance + 1e-05) * gain[...]
    normed = jnp.concatenate([normed, jnp.zeros_like(normed)], axis=0).astype(BF)
    queries = dot(normed, qw[...])[0:8]
    key_value = dot(normed, kvw[...])[0:8]
    qbuf[0] = jnp.concatenate([queries[:, i * 128:i * 128 + 128] for i in range(2)], axis=0).astype(BF)
    kvbuf[0] = jnp.concatenate([key_value[:, i * 128:i * 128 + 128] for i in range(4)], axis=0).astype(BF)

    q_all = pltpu.make_async_copy(qbuf.at[pl.ds(1, n_row - 1)], qbuf.at[pl.ds(1, n_row - 1)], gr.at[0])
    kv_all = pltpu.make_async_copy(kvbuf.at[pl.ds(1, n_col - 1)], kvbuf.at[pl.ds(1, n_col - 1)], gr.at[1])
    q_gone = pltpu.make_async_copy(qbuf.at[pl.ds(1, n_row - 1)], qbuf.at[pl.ds(1, n_row - 1)], gs.at[0])
    kv_gone = pltpu.make_async_copy(kvbuf.at[pl.ds(1, n_col - 1)], kvbuf.at[pl.ds(1, n_col - 1)], gs.at[1])
    sends = [(n / len(row_far), qbuf, 0, i, row_peer(i)) for n, i in enumerate(row_far)]
    sends += [(n / len(col_far), kvbuf, 1, i, col_peer(i)) for n, i in enumerate(col_far)]
    for _, buf, n, i, peer in sorted(sends, key=lambda s: s[0]):
        pltpu.make_async_remote_copy(src_ref=buf.at[0], dst_ref=buf.at[i], send_sem=gs.at[n], recv_sem=gr.at[n],
                                     device_id=peer, device_id_type=MESH).start()
    pack_rows(enc, rows_e)
    pack_ends(enc, enc_s)
    enc_copies = halo_copies(enc, rows_e, enc_lo, enc_hi, es, er, enc_s, enc_r)
    start_all(enc_copies)
    spread_taps(wout)

    q_all.wait()
    kv_all.wait()
    n_keys = n_col * 16
    lane_group = iota((n_keys, 128), 1) // 32
    keys = kvbuf[:, 0:16, :].reshape(n_keys, 128)
    values = kvbuf[:, 16:32, :].reshape(n_keys, 128)
    for g in range(4):
        mine = (lane_group == g).astype(F32).astype(BF)
        kmask[g] = keys * mine
        vmask[g, :, 0:128] = values * mine
        vmask[g, :, 128:256] = mine
    slots = min(8, n_row)
    n_rows = slots * 16
    same_half = (iota((n_rows, n_keys), 0) // 8) % 2 == (iota((n_rows, n_keys), 1) // 8) % 2
    group = iota((n_rows, 128), 1) // 32
    compact = iota((slots, 16, 128), 1) == iota((slots, 16, 128), 2) % 32

    def attend(i):
        at = slice(i * slots, i * slots + slots)
        query = qbuf[at].reshape(n_rows, 128)
        total, peaks = jnp.zeros((n_rows, 256), F32), jnp.zeros((n_rows, 128), F32)
        for g in range(4):
            scores = lax.dot_general(query, kmask[g], (((1,), (1,)), ((), ())), preferred_element_type=F32)
            scores = jnp.where(same_half, scores * 32 ** (-0.5), -1e30)
            peak = jnp.max(scores, axis=1, keepdims=True)
            total = total + dot(jnp.exp(scores - peak).astype(BF), vmask[g])
            peaks = jnp.where(group == g, peak, peaks)
        weight = total[:, 128:256]
        osend[at] = (total[:, 0:128] / weight).astype(BF).reshape(slots, 16, 128)
        level = (peaks + jnp.log(weight)).reshape(slots, 16, 128)
        lsend[at] = jnp.sum(jnp.where(compact, level, 0.0), axis=1, keepdims=True)

    others = pl.ds(1, n_row - 1)
    n_blocks = n_row // slots
    for block in sorted(range(n_blocks), key=lambda k: -min(k, n_blocks - k)):
        attend(block)
        for i in [i for i in row_far if i // slots == block]:
            for n, (src, dst) in enumerate(((osend, orecv), (lsend, lrecv))):
                pltpu.make_async_remote_copy(src_ref=src.at[i], dst_ref=dst.at[i], send_sem=rs.at[n], recv_sem=rr.at[n],
                                             device_id=row_peer(i, -1), device_id_type=MESH).start()
    orecv[0] = osend[0]
    lrecv[0] = lsend[0]
    arrived(enc_copies)
    unpack_ends(enc, enc_r)
    pltpu.make_async_copy(orecv.at[others], orecv.at[others], rr.at[0]).wait()
    pltpu.make_async_copy(lrecv.at[others], lrecv.at[others], rr.at[1]).wait()

    levels = lrecv[...]
    share = jnp.exp(levels - jnp.max(levels, axis=0, keepdims=True))
    share = share / jnp.sum(share, axis=0, keepdims=True)
    spot = iota((n_row, 16, 128), 1) == iota((n_row, 16, 128), 2) % 32
    share = jnp.where(spot, share, 0.0).reshape(n_row * 16, 128)
    high = share.astype(BF)
    low = (share - high.astype(F32)).astype(BF)
    blocks = ((iota((256, 128), 0) % 128) // 32 == iota((256, 128), 1) // 32).astype(F32).astype(BF)
    share = dot(jnp.concatenate([high, low], axis=1), blocks).reshape(n_row, 16, 128)
    attended = jnp.sum(share * orecv[...].astype(F32), axis=0)
    attended = jnp.concatenate([attended[0:8], attended[8:16]], axis=1)
    attended = jnp.concatenate([attended, jnp.zeros_like(attended)], axis=0).astype(BF)
    mixture = tokens_s[...] + dot(attended, ow[...])[0:8]
    mixture = jnp.concatenate([mixture, jnp.zeros_like(mixture)], axis=0).astype(BF)
    r, k = iota((16, 16), 0), iota((16, 16), 1)
    twice = ((r // 8) * 4 + (r % 8) // 2 == k).astype(F32).astype(BF)
    upward = dot(dot(twice, mixture).astype(BF), uw[...])
    odd, right = row8 % 2 == 1, group8 >= 2
    for a in range(2):
        first = upward[0:8, a * 128:a * 128 + 128]
        second = upward[8:16, a * 128:a * 128 + 128]
        plane = jnp.where(right, jnp.where(odd, second, roll(second, 64, 1)), jnp.where(odd, roll(first, 64, 1), first))
        for y in range(8):
            up[a, y, 0] = plane[y:y + 1, :]
            uppad[1 + a, 1 + y, 1] = plane[y:y + 1, :]

    up_copies = []
    for n, (a, b, c) in enumerate(STEPS):
        sx = {-1: pl.ds(0, 1), 0: pl.ds(0, 2), 1: pl.ds(1, 1)}[a]
        dx = {-1: pl.ds(3, 1), 0: pl.ds(1, 2), 1: pl.ds(0, 1)}[a]
        sy = {-1: pl.ds(0, 1), 0: pl.ds(0, 8), 1: pl.ds(7, 1)}[b]
        dy = {-1: pl.ds(9, 1), 0: pl.ds(1, 8), 1: pl.ds(0, 1)}[b]
        up_copies.append(remote(up.at[sx, sy, pl.ds(0, 1)], uppad.at[dx, dy, pl.ds(1 - c, 1)], us.at[n], ur.at[n], (a, b, c)))
    start_all(up_copies)
    departed(vol_copies)
    departed(enc_copies)
    departed(up_copies)
    q_gone.wait()
    kv_gone.wait()
    pltpu.make_async_copy(orecv.at[others], orecv.at[others], rs.at[0]).wait()
    pltpu.make_async_copy(lrecv.at[others], lrecv.at[others], rs.at[1]).wait()

    group1 = iota((1, 128), 1) // 32

    def middle(plane, y):
        here = uppad[plane, y, 1]
        parts = []
        for q in range(4):
            part = jnp.where(group1 == q, here, 0.0)
            part = part + roll(part, 64, 1)
            parts.append(part + roll(part, 32, 1))
        return jnp.concatenate(parts, axis=1)

    def wide(plane, y):
        return jnp.concatenate([uppad[plane, y, 0], middle(plane, y), uppad[plane, y, 2]], axis=1)

    def side(n):
        return lambda plane, y: uppad[plane, y, n]

    def join_planes(planes, first, width, row_of):
        row = iota((8, width), 0)
        for plane in planes:
            xs = (range(0, 1), range(1, 5), range(5, 9), range(9, 10))[plane]
            for y2 in range(2):
                four = [row_of(plane, 1 + 4 * y2 + i) for i in range(4)]
                more = jnp.concatenate([jnp.where(row < 4, four[2 * i], four[2 * i + 1]) for i in range(2)], axis=0)
                for x in xs:
                    here = (x, slice(16 * y2, 16 * y2 + 16), slice(first, first + width))
                    joi[here] = (enc[here].astype(F32) + more).astype(BF)

    join_planes((1, 2), 128, 512, middle)
    lay_own(joi)
    arrived(up_copies)
    join_planes((1, 2), 0, 128, side(0))
    join_planes((1, 2), 640, 128, side(2))
    join_planes((0, 3), 0, 768, wide)
    row_rim = iota((16, 768), 0)
    for rim, full, y in ((enc_lo, joi_lo, 0), (enc_hi, joi_hi, 9)):
        planes = [wide(plane, y) for plane in range(4)]
        full[0] = (rim[0].astype(F32) + planes[0]).astype(BF)
        full[1] = (rim[1].astype(F32) + jnp.where(row_rim < 4, planes[1], planes[2])).astype(BF)
        full[2] = (rim[2].astype(F32) + planes[3]).astype(BF)

    def keep_result(x, h, value):
        out_ref[x, :, 256 * h:256 * h + 256] = value.astype(BF)

    convolve(joi, joi_lo, joi_hi, keep_result)


def on_device(sizes, volume, conv_in, conv_out, norm_gain, q_weight, kv_weight, out_weight, up_weight):
    n_row, n_col = (sizes[1] // 2) * sizes[2], sizes[0] * 2
    padded, rim, rows = (10, 32, 768), (3, 16, 768), (2, 16, 512)
    vmem = pltpu.VMEM
    scratch = [vmem((8, 32, 16, 32), BF)] + [vmem(padded, BF), vmem(rim, BF), vmem(rim, BF)] * 3 + [vmem(rows, BF)] * 2 + [vmem((2, 2, 32, 128), BF)] * 4
    scratch += [vmem((864, 32), BF)] * 2 + [vmem((1, 256), F32), vmem((256, 256), BF), vmem((256, 512), BF), vmem((256, 256), BF), vmem((256, 256), BF)]
    scratch += [vmem((3, 1024, 256), BF), vmem((544, 1024), BF), vmem((3, 552, 256), F32), vmem((8, 256), F32)]
    scratch += [vmem((n_row, 16, 128), BF), vmem((n_col, 32, 128), BF), vmem((4, n_col * 16, 128), BF), vmem((4, n_col * 16, 256), BF)]
    scratch += [vmem((n_row, 16, 128), BF)] * 2 + [vmem((n_row, 1, 128), F32)] * 2
    scratch += [vmem((2, 8, 1, 1, 128), F32), vmem((4, 10, 3, 1, 128), F32)]
    dma = pltpu.SemaphoreType.DMA
    scratch += [dma((8,))] + [dma((26,))] * 6 + [dma((2,))] * 4
    result = pl.pallas_call(
        functools.partial(kernel, sizes),
        out_shape=jax.ShapeDtypeStruct((8, 32, 512), BF),
        in_specs=[pl.BlockSpec(memory_space=pltpu.HBM)] * 8,
        out_specs=pl.BlockSpec(memory_space=pltpu.VMEM),
        scratch_shapes=scratch,
        compiler_params=pltpu.CompilerParams(collective_id=0, has_side_effects=True, vmem_limit_bytes=48 * 2**20),
    )(*(pltpu.with_memory_space_constraint(a, pltpu.HBM) for a in (volume, conv_in.reshape(864, 32), conv_out.reshape(864, 32), norm_gain.reshape(1, 256), q_weight, kv_weight, out_weight, up_weight)))
    return result.reshape(8, 32, 16, 32)


def solution(mesh):
    placed = (P("gx", "gy", "gz", None), P(), P(), P(), P(), P(), P(), P())
    sizes = tuple(mesh.shape[name] for name in ("gx", "gy", "gz"))
    return jax.shard_map(
        functools.partial(on_device, sizes), mesh=mesh, in_specs=placed, out_specs=P("gx", "gy", "gz", None), check_vma=False
    )
```
